768 devices in a mesh: lat: 96 (over x, z, core), lon: 8 (over y).
Axes of the slice: x: 4, y: 8, z: 12, core: 2. Of those that a mesh axis runs over, the one named last changes fastest.
Arguments:
- wind_u: float32 [8, 1536, 2560], P(None, 'lat', 'lon'), may hold values from -6 to 6
- wind_v: float32 [8, 1536, 2560], P(None, 'lat', 'lon'), may hold values from -6 to 6
- basis: bfloat16 [864, 640, 768], P('lat'), may hold values from -6 to 6
- wave_slots: int32 [640], replicated, may hold values from 0 to 863, as said below
- degree_count: int32 [640], replicated, may hold values from 1 to 640, as said below
- viscosity: float32 [8], replicated, may hold values from 0.5 to 50
Outputs:
- spectral: float32 [864, 8, 2, 2, 640], P('lat', 'lon')
- tendency: float32 [8, 2, 1536, 2560], P(None, None, 'lat', 'lon')
The draws below stay inside these ranges and needn't reach their ends.
Inputs may be any that keep to these rules, and one draw needn't show every extreme that they name: `wave_slots`: all values differ; slot s belongs to owner s // 9, so an owner holds at most 9 wavenumbers, and one owner holds exactly 9. degree_count[0] = 640, and degree_count[m] <= 640 - m.
All inputs are finite; a program needn't handle non-finite values.
Results may differ from the reference program's by a relative error of at most 0.0048.
Values may be sent and summed in bfloat16 or wider, within the bound.
A program may use at most 128 MiB of HBM per device.

```python
import math
import jax
import jax.numpy as jnp
from jax import lax

NLAT = 1536
NLON = 2560
TRUNC = 640
LEV = 8
CAP = 9
SLOTS = 864


def draw_wave_slots(key, part):
    base = jax.random.fold_in(key, 7)
    owner_key, order_key = jax.random.split(base)
    full_owner = jax.random.randint(owner_key, (), 0, SLOTS // CAP)
    ranking = jax.random.permutation(order_key, SLOTS)
    owners = jnp.arange(SLOTS) // CAP
    priority = jnp.where(owners == full_owner, -1, ranking)
    chosen = jnp.argsort(priority, stable=True)
    return chosen[:TRUNC].astype(jnp.int32)


def draw_degree_count(key, part):
    base = jax.random.fold_in(key, 13)
    shortening = jax.random.randint(base, (TRUNC,), 0, 32)
    shortening = shortening.at[0].set(0)
    wave_ids = jnp.arange(TRUNC)
    return jnp.maximum(1, TRUNC - wave_ids - shortening).astype(jnp.int32)


def block_levels(stream_key, extent, pieces, smallest, largest):
    def one(axis_at, blocks):
        heights = jax.random.uniform(jax.random.fold_in(jax.random.fold_in(stream_key, 6), axis_at), (blocks,), jnp.float32, smallest / len(pieces), largest / len(pieces))
        return jnp.repeat(jnp.exp(heights), extent[axis_at] // blocks).reshape((-1,) + (1,) * (len(extent) - axis_at - 1))

    loudness = one(*pieces[0])
    for cut in pieces[1:]:
        loudness = loudness * one(*cut)
    return loudness


def normal_values(own_key, shape, deviation, limit, pieces=(), kind=jnp.bfloat16):
    factor_of = block_levels(own_key, shape, pieces, -0.22, 0.18) if pieces else 1.0
    drawn = jax.random.normal(own_key, shape, jnp.float32) * deviation * factor_of
    return jnp.minimum(jnp.maximum(drawn, -limit), limit).astype(kind)


def setup_inputs(seed: int = 0) -> dict:
    key_of = jax.random.split(jax.random.key(seed), 7)
    wind_u = normal_values(key_of[0], (LEV, NLAT, NLON), 1.0, 6.0, ((1, 96), (2, 8)), jnp.float32)
    wind_v = normal_values(key_of[1], (LEV, NLAT, NLON), 1.0, 6.0, ((1, 96), (2, 8)), jnp.float32)
    basis = normal_values(key_of[2], (SLOTS, TRUNC, NLAT // 2), 1.0, 6.0, ((0, 96),))
    wave_slots = draw_wave_slots(jax.random.fold_in(key_of[6], 71), 0)
    degree_count = draw_degree_count(jax.random.fold_in(key_of[6], 71), 0)
    viscosity = jnp.clip(jnp.exp(jax.random.uniform(key_of[5], (LEV,), jnp.float32, math.log(0.5), math.log(50.0))), 0.5, 50.0)
    return dict(wind_u=wind_u, wind_v=wind_v, basis=basis, wave_slots=wave_slots, degree_count=degree_count, viscosity=viscosity)


def reference(wind_u, wind_v, basis, wave_slots, degree_count, viscosity):
    products = jnp.stack([wind_u * wind_v, wind_u * wind_u - wind_v * wind_v], axis=1)
    spectrum = jnp.fft.rfft(products, axis=-1)[..., :TRUNC] / math.sqrt(NLON)
    fourier = jnp.stack([jnp.real(spectrum), jnp.imag(spectrum)], axis=-1).astype(jnp.float32)
    fourier = lax.optimization_barrier(fourier.astype(jnp.bfloat16))
    by_wave = jnp.transpose(fourier, (3, 0, 1, 2, 4))
    slot_fourier = jnp.zeros((SLOTS,) + by_wave.shape[1:], jnp.bfloat16).at[wave_slots].set(by_wave)
    wave_ids = jnp.arange(TRUNC, dtype=jnp.int32)
    wave_of_slot = jnp.zeros((SLOTS,), jnp.int32).at[wave_slots].set(wave_ids)
    count_of_slot = jnp.zeros((SLOTS,), jnp.int32).at[wave_slots].set(degree_count.astype(jnp.int32))
    degree_ids = jnp.arange(TRUNC, dtype=jnp.int32)
    parity = jnp.where(degree_ids % 2 == 0, 1.0, -1.0).astype(jnp.float32)

    def per_slot(packed):
        basis_rows, slot_rows, wavenumber, kept_count = packed
        north = basis_rows.astype(jnp.float32)
        basis_wide = jnp.concatenate([north, parity[:, None] * north[:, ::-1]], axis=1)
        raw_coeffs = jnp.einsum('lfar,ja->lfrj', slot_rows.astype(jnp.float32), basis_wide) * (1.0 / math.sqrt(NLAT))
        total_degree = wavenumber + degree_ids
        scaled = (total_degree * (total_degree + 1)).astype(jnp.float32) / float(TRUNC * (TRUNC + 1))
        damping = 1.0 / (1.0 + viscosity[:, None, None, None] * (scaled * scaled)[None, None, None, :])
        damped = jnp.where((degree_ids < kept_count)[None, None, None, :], raw_coeffs * damping, jnp.float32(0.0))
        rounded = lax.optimization_barrier(damped.astype(jnp.bfloat16))
        back_rows = jnp.einsum('lfrj,ja->lfar', rounded.astype(jnp.float32), basis_wide) * (1.0 / math.sqrt(TRUNC))
        return (damped, back_rows.astype(jnp.bfloat16))
    spectral, returned = lax.map(per_slot, (basis, slot_fourier, wave_of_slot, count_of_slot))
    by_slot = returned[wave_slots]
    back_wave = jnp.transpose(by_slot, (1, 2, 3, 0, 4)).astype(jnp.float32)
    complex_rows = back_wave[..., 0] + 1j * back_wave[..., 1]
    padded = jnp.pad(complex_rows, ((0, 0), (0, 0), (0, 0), (0, NLON // 2 + 1 - TRUNC)))
    tendency = (jnp.fft.irfft(padded, n=NLON, axis=-1) * math.sqrt(NLON)).astype(jnp.float32)
    return (spectral, tendency)
```

```python
import functools
import math

import jax
import jax.numpy as jnp
import ml_dtypes
import numpy as np
from jax import lax
from jax.experimental import pallas as pl
from jax.experimental.pallas import tpu as pltpu
from jax.sharding import PartitionSpec as P

MESH = pl.DeviceIdType.MESH
F32 = jnp.float32
BF16 = jnp.bfloat16

NX, NZ, NC = 4, 12, 2
GROUPS = NX * NC
SECTORS = 8
ROWS = 48
HALF = math.sqrt(0.5)


def nt(a, b):
    return lax.dot_general(a, b, (((1,), (1,)), ((), ())), preferred_element_type=F32)


def nn(a, b):
    return lax.dot_general(a, b, (((1,), (0,)), ((), ())), preferred_element_type=F32)


def tn(a, b):
    return lax.dot_general(a, b, (((0,), (0,)), ((), ())), preferred_element_type=F32)


@functools.cache
def wave_lanes(waves):
    per = waves // SECTORS
    out = np.full((4, 256), -1, np.int64)
    for j in range(4):
        other = 4 if j == 0 else SECTORS - j
        out[j, :per] = SECTORS * np.arange(per) + j
        out[j, per : 2 * per] = SECTORS * np.arange(per) + other
    return out


@functools.cache
def dft_table(length, waves):
    sector = length // SECTORS
    per = waves // SECTORS
    lanes = wave_lanes(waves)
    t = np.arange(sector)
    table = np.zeros((4, 2, sector, 2, 256), np.float64)
    for j in range(4):
        m = lanes[j, : 2 * per]
        angle = 2.0 * math.pi * ((t[:, None] * m[None, :]) % length) / length
        c, s = np.cos(angle), np.sin(angle)
        if j == 0:
            table[j, 0, :, 0, :per] = c[:, :per]
            table[j, 0, :, 1, :per] = -s[:, :per]
            table[j, 1, :, 0, per : 2 * per] = c[:, per:]
            table[j, 1, :, 1, per : 2 * per] = -s[:, per:]
        else:
            sign = np.where(np.arange(2 * per) < per, 1.0, -1.0)
            table[j, 0, :, 0, : 2 * per] = c
            table[j, 0, :, 1, : 2 * per] = -s
            table[j, 1, :, 0, : 2 * per] = s * sign
            table[j, 1, :, 1, : 2 * per] = c * sign
    table = table.reshape(4, 2 * sector, 512) / math.sqrt(length)
    high = table.astype(ml_dtypes.bfloat16)
    low = (table - high.astype(np.float64)).astype(ml_dtypes.bfloat16)
    return high, low


@functools.cache
def spread_table(cap):
    e = np.zeros((NZ, ROWS, 4, 128), np.float32)
    for z in range(NZ):
        for k in range(cap):
            for f in range(2):
                for r in range(2):
                    e[z, k * 4 + f * 2 + r, r * 2 + f, z * cap + k] = 1.0
    return e.reshape(NZ * ROWS, 512).astype(ml_dtypes.bfloat16)


@functools.cache
def lane_table():
    p = np.zeros((512, 512), np.float32)
    for z in range(4):
        for x in range(NX):
            for c in range(NC):
                for i in range(16):
                    lane = z * 32 + c * 16 + i
                    if x >= NX // 2:
                        lane = 127 - lane
                    p[z * 128 + (x * NC + c) * 16 + i, x * 128 + lane] = 1.0
    return p.astype(ml_dtypes.bfloat16)


def kernel(
    u_ref, v_ref, tgt_ref, ws_ref, cnt_ref, visc_ref, basis_hbm, hi_hbm, lo_hbm, e_hbm, pi_hbm,
    spec_ref, tend_ref,
    basis, hi, lo, e_tab, pi_tab, onehot, damp,
    send_l, recv_l, send_a, recv_a, send_b, recv_b, turned,
    back_t, send_b2, recv_b2, send_a2, recv_a2, send_l2, recv_l2,
    load_sem, sl, rl, sa, ra, sb, rb, sb2, rb2, sa2, ra2, sl2, rl2,
):
    lat = lax.axis_index("lat")
    lon = lax.axis_index("lon")
    x = lat // (NZ * NC)
    z = lat // NC % NZ
    core = lat % NC
    group = x * NC + core
    cap, degrees, half_lat = basis.shape
    waves = ws_ref.shape[1]
    sector = u_ref.shape[2]

    def in_group(g):
        return ((g // NC) * (NZ * NC) + z * NC + g % NC, lon)

    def in_column(zz):
        return (x * (NZ * NC) + zz * NC + core, lon)

    def in_sector(s):
        return (lat, s)

    barrier = pltpu.get_barrier_semaphore()

    def greet(device_of, me, n):
        def one(d, carry):
            pl.semaphore_signal(barrier, inc=1, device_id=device_of((me + d) % n), device_id_type=MESH)
            return carry

        lax.fori_loop(1, n, one, 0)

    greet(in_sector, lon, SECTORS)
    greet(in_group, group, GROUPS)
    greet(in_column, z, NZ)

    loads = [
        pltpu.make_async_copy(src, dst, load_sem.at[i])
        for i, (src, dst) in enumerate(
            ((hi_hbm, hi), (lo_hbm, lo), (e_hbm, e_tab), (pi_hbm, pi_tab), (basis_hbm, basis))
        )
    ]
    for load in loads:
        load.start()

    def products(level, carry):
        u = u_ref[level]
        v = v_ref[level]
        send_l[level, 0] = u * v
        send_l[level, 1] = u * u - v * v
        return carry

    lax.fori_loop(0, SECTORS, products, 0)
    recv_l[lon] = send_l[lon]
    pl.semaphore_wait(barrier, SECTORS + GROUPS + NZ - 3)

    def exchange(src, dst, send_sem, recv_sem, device_of, me, n):
        def copy(d):
            to = (me + d) % n
            return pltpu.make_async_remote_copy(
                src_ref=src.at[to],
                dst_ref=dst.at[me],
                send_sem=send_sem.at[d],
                recv_sem=recv_sem.at[d],
                device_id=device_of(to),
                device_id_type=MESH,
            )

        def start():
            def one(d, carry):
                copy(d).start()
                return carry

            lax.fori_loop(1, n, one, 0)

        def wait():
            def one(d, carry):
                copy(d).wait()
                return carry

            lax.fori_loop(1, n, one, 0)

        return start, wait

    start, wait = exchange(send_l, recv_l, sl, rl, in_sector, lon, SECTORS)
    start()

    target = tgt_ref[...]
    for b in range(GROUPS):
        ids = lax.broadcasted_iota(jnp.int32, (128, 1024), 0) + b * 128
        onehot[pl.ds(b * 128, 128), :] = jnp.where(ids == target, 1.0, 0.0).astype(BF16)

    rows40 = damp.shape[0]
    slot = lax.broadcasted_iota(jnp.int32, (rows40, waves), 0) // 4
    here = (ws_ref[...] == lat * cap + slot) & (slot < cap)
    wave_ids = lax.broadcasted_iota(jnp.int32, (rows40, waves), 1)
    wave_here = jnp.sum(jnp.where(here, wave_ids, 0).astype(F32), axis=1, keepdims=True)
    kept_here = jnp.sum(jnp.where(here, cnt_ref[...], 0).astype(F32), axis=1, keepdims=True)
    levels = lax.broadcasted_iota(jnp.int32, (1, SECTORS), 1)
    rate = jnp.sum(jnp.where(levels == lon, visc_ref[...], 0.0), axis=1, keepdims=True)
    degree = lax.broadcasted_iota(jnp.int32, (rows40, degrees), 1).astype(F32)
    total = wave_here + degree
    q = total * (total + 1.0) / float(degrees * (degrees + 1))
    damping = (1.0 / math.sqrt(2 * half_lat)) / (1.0 + rate * (q * q))
    damp[...] = jnp.where(degree < kept_here, damping, 0.0)

    wait()
    loads[0].wait()
    loads[1].wait()

    sums = []
    for f in range(2):
        a = [recv_l[s, f] for s in range(SECTORS)]
        e0, e1, e2, e3 = (a[i] + a[i + 4] for i in range(4))
        o0, o1, o2, o3 = (a[i] - a[i + 4] for i in range(4))
        od = HALF * (o1 - o3)
        os = HALF * (o1 + o3)
        sums.append(
            (
                (e0 + e1 + e2 + e3, e0 - e1 + e2 - e3),
                (o0 + od, -(os + o2)),
                (e0 - e2, e3 - e1),
                (o0 - od, o2 - os),
            )
        )
    for j in range(4):
        both = jnp.concatenate(
            [jnp.concatenate([sums[f][j][0], sums[f][j][1]], axis=1) for f in range(2)], axis=0
        )
        high = both.astype(BF16)
        low = (both - high.astype(F32)).astype(BF16)
        two = nn(jnp.concatenate([high, low], axis=0), hi[j])
        four = two[:32] + two[32:] + nn(high, lo[j])
        turned[0:32, pl.ds(j * 256, 256)] = four[:, :256].astype(BF16)
        turned[32:64, pl.ds(j * 256, 256)] = four[:, 256:].astype(BF16)

    placed = nt(turned[...], onehot[...]).astype(BF16)
    for g in range(GROUPS):
        for b in range(4):
            send_a[g, :, pl.ds(b * 128, 128)] = placed[b * 16 : b * 16 + 16, g * 128 : g * 128 + 128]
    start, wait = exchange(send_a, recv_a, sa, ra, in_group, group, GROUPS)
    start()
    recv_a[group] = send_a[group]
    loads[2].wait()
    wait()
    spread = nt(e_tab[...], recv_a[...].reshape(GROUPS * 16, 512)).astype(BF16)
    send_b[...] = spread.reshape(NZ, ROWS, 128)
    start, wait = exchange(send_b, recv_b, sb, rb, in_column, z, NZ)
    start()
    recv_b[z] = send_b[z]
    loads[3].wait()
    loads[4].wait()
    wait()

    quarters = NZ // 4
    gathered = jnp.concatenate(
        [
            jnp.concatenate([recv_b[4 * i + k] for k in range(4)], axis=1)
            for i in range(quarters)
        ],
        axis=0,
    )
    natural = nn(gathered, pi_tab[...])
    parity = jnp.where(lax.broadcasted_iota(jnp.int32, (8, degrees), 1) % 2 == 0, 1.0, -1.0)
    first = lax.broadcasted_iota(jnp.int32, (8, 1), 0) < 4
    blocks = half_lat // 128
    for i in range((cap + 1) // 2):
        r0 = 8 * i
        north, south = [], []
        for b in range(blocks):
            xx, gg = b // quarters, b % quarters
            north.append(natural[gg * ROWS + r0 : gg * ROWS + r0 + 8, xx * 128 : xx * 128 + 128])
            xx, gg = NX - 1 - xx, quarters - 1 - gg
            south.append(natural[gg * ROWS + r0 : gg * ROWS + r0 + 8, xx * 128 : xx * 128 + 128])
        both = jnp.concatenate(
            [jnp.concatenate(north, axis=1), jnp.concatenate(south, axis=1)], axis=0
        ).astype(BF16)
        raws = []
        for k in (2 * i, 2 * i + 1):
            if k < cap:
                out = nt(both, basis[k])
                raws.append(out[:8] + parity * out[8:])
        raw = jnp.where(first, raws[0], raws[1] if len(raws) > 1 else 0.0)
        spectral = raw * damp[pl.ds(r0, 8), :]
        for k in (2 * i, 2 * i + 1):
            if k < cap:
                at = 4 * (k - 2 * i)
                for f in range(2):
                    spec_ref[k, 0, f] = spectral[at + 2 * f : at + 2 * f + 2]
        rounded = spectral.astype(BF16).astype(F32)
        pair = jnp.concatenate([rounded, rounded * parity], axis=0).astype(BF16)
        outs = [nn(pair, basis[k]) for k in (2 * i, 2 * i + 1) if k < cap]
        keep = jnp.concatenate([first, first], axis=0)
        back = jnp.where(keep, outs[0], outs[1] if len(outs) > 1 else 0.0)
        back = back * (1.0 / math.sqrt(degrees))
        for b in range(blocks):
            xx, gg = b // quarters, b % quarters
            back_t[pl.ds(gg * ROWS + r0, 8), pl.ds(xx * 128, 128)] = back[:8, b * 128 : b * 128 + 128]
            xx, gg = NX - 1 - xx, quarters - 1 - gg
            back_t[pl.ds(gg * ROWS + r0, 8), pl.ds(xx * 128, 128)] = back[8:, b * 128 : b * 128 + 128]
    for gg in range(quarters):
        back_t[pl.ds(gg * ROWS + 40, 8), :] = jnp.zeros((8, 512), F32)

    mixed = nt(back_t[...].astype(BF16), pi_tab[...]).astype(BF16)
    for zz in range(NZ):
        send_b2[zz] = mixed[zz // 4 * ROWS : zz // 4 * ROWS + ROWS, zz % 4 * 128 : zz % 4 * 128 + 128]
    start, wait = exchange(send_b2, recv_b2, sb2, rb2, in_column, z, NZ)
    start()
    recv_b2[z] = send_b2[z]
    wait()
    joined = tn(recv_b2[...].reshape(NZ * ROWS, 128), e_tab[...]).astype(BF16)
    send_a2[...] = joined.reshape(GROUPS, 16, 512)
    start, wait = exchange(send_a2, recv_a2, sa2, ra2, in_group, group, GROUPS)
    start()
    recv_a2[group] = send_a2[group]
    wait()

    by_part = jnp.concatenate(
        [
            jnp.concatenate([recv_a2[g, :, pl.ds(b * 128, 128)] for g in range(GROUPS)], axis=1)
            for b in range(4)
        ],
        axis=0,
    )
    waved = nn(by_part, onehot[...])
    weight = jnp.where(lax.broadcasted_iota(jnp.int32, (1, 1024), 1) == 0, 1.0, 2.0)
    waved = (waved * weight).astype(BF16)
    parts = []
    for j in range(4):
        lhs = jnp.concatenate(
            [waved[:32, j * 256 : j * 256 + 256], waved[32:, j * 256 : j * 256 + 256]], axis=1
        )
        out = nt(lhs, hi[j]) + nt(lhs, lo[j])
        parts.append((out[:, :sector], out[:, sector:]))
    (u0, u4), (u1, v1), (u2, v2), (u3, v3) = parts
    even, odd = u0 + u4, u0 - u4
    ud, us = HALF * (u1 - u3), u1 + u3
    vd, vs = v1 - v3, HALF * (v1 + v3)
    grid = (
        even + us + u2,
        odd + ud - vs - v2,
        even - u2 - vd,
        odd - ud - vs + v2,
        even - us + u2,
        odd - ud + vs - v2,
        even - u2 + vd,
        odd + ud + vs + v2,
    )
    for s in range(SECTORS):
        send_l2[s] = grid[s].astype(BF16)
    start, wait = exchange(send_l2, recv_l2, sl2, rl2, in_sector, lon, SECTORS)
    start()
    recv_l2[lon] = send_l2[lon]
    wait()
    for s in range(SECTORS):
        tend_ref[s] = recv_l2[s].astype(F32).reshape(2, 16, sector)


def body(wind_u, wind_v, basis, wave_slots, degree_count, viscosity):
    levels, lat_rows, sector = wind_u.shape
    cap, degrees, half_lat = basis.shape
    waves = wave_slots.shape[0]
    per = waves // SECTORS
    high, low = dft_table(sector * SECTORS, waves)
    owner = wave_slots // cap
    lane = (owner // (NZ * NC) * NC + owner % NC) * 128 + owner // NC % NZ * cap + wave_slots % cap
    by_residue = lane.reshape(per, SECTORS).T
    fill = jnp.full((256 - 2 * per,), -1, jnp.int32)
    target = jnp.concatenate(
        [
            part
            for j in range(4)
            for part in (by_residue[j], by_residue[4 if j == 0 else SECTORS - j], fill)
        ]
    ).reshape(1, 1024)
    vmem = pl.BlockSpec(memory_space=pltpu.VMEM)
    hbm = pl.BlockSpec(memory_space=pl.ANY)
    dma = pltpu.SemaphoreType.DMA
    return pl.pallas_call(
        kernel,
        out_shape=(
            jax.ShapeDtypeStruct((cap, 1, 2, 2, degrees), F32),
            jax.ShapeDtypeStruct((levels, 2, lat_rows, sector), F32),
        ),
        in_specs=[vmem] * 6 + [hbm] * 5,
        out_specs=(vmem, vmem),
        scratch_shapes=[
            pltpu.VMEM(basis.shape, BF16),
            pltpu.VMEM(high.shape, BF16),
            pltpu.VMEM(low.shape, BF16),
            pltpu.VMEM((NZ * ROWS, 512), BF16),
            pltpu.VMEM((512, 512), BF16),
            pltpu.VMEM((1024, 1024), BF16),
            pltpu.VMEM((40, degrees), F32),
            pltpu.VMEM((SECTORS, 2, lat_rows, sector), F32),
            pltpu.VMEM((SECTORS, 2, lat_rows, sector), F32),
            pltpu.VMEM((GROUPS, 16, 512), BF16),
            pltpu.VMEM((GROUPS, 16, 512), BF16),
            pltpu.VMEM((NZ, ROWS, 128), BF16),
            pltpu.VMEM((NZ, ROWS, 128), BF16),
            pltpu.VMEM((64, 1024), BF16),
            pltpu.VMEM((NZ // 4 * ROWS, 512), F32),
            pltpu.VMEM((NZ, ROWS, 128), BF16),
            pltpu.VMEM((NZ, ROWS, 128), BF16),
            pltpu.VMEM((GROUPS, 16, 512), BF16),
            pltpu.VMEM((GROUPS, 16, 512), BF16),
            pltpu.VMEM((SECTORS, 2 * lat_rows, sector), BF16),
            pltpu.VMEM((SECTORS, 2 * lat_rows, sector), BF16),
            dma((5,)),
        ]
        + [dma((n,)) for n in (8, 8, 8, 8, 12, 12, 12, 12, 8, 8, 8, 8)],
        compiler_params=pltpu.CompilerParams(
            collective_id=0, has_side_effects=True, vmem_limit_bytes=48 * 2**20
        ),
    )(
        wind_u,
        wind_v,
        target,
        wave_slots.reshape(1, waves),
        degree_count.reshape(1, waves),
        viscosity.reshape(1, levels),
        basis,
        jnp.asarray(high),
        jnp.asarray(low),
        jnp.asarray(spread_table(cap)),
        jnp.asarray(lane_table()),
    )


def solution(mesh):
    return jax.shard_map(
        body,
        mesh=mesh,
        in_specs=(
            P(None, "lat", "lon"),
            P(None, "lat", "lon"),
            P("lat", None, None),
            P(),
            P(),
            P(),
        ),
        out_specs=(P("lat", "lon", None, None, None), P(None, None, "lat", "lon")),
        check_vma=False,
    )
```

```python
import functools
import math

import jax
import jax.numpy as jnp
import ml_dtypes
import numpy as np
from jax import lax
from jax.experimental import pallas as pl
from jax.experimental.pallas import tpu as pltpu
from jax.sharding import PartitionSpec as P

MESH = pl.DeviceIdType.MESH
F32 = jnp.float32
BF16 = jnp.bfloat16

NX, NZ, NC = 4, 12, 2
GROUPS = NX * NC
SECTORS = 8
ROWS = 48
HALF = math.sqrt(0.5)


def nt(a, b):
    return lax.dot_general(a, b, (((1,), (1,)), ((), ())), preferred_element_type=F32)


def nn(a, b):
    return lax.dot_general(a, b, (((1,), (0,)), ((), ())), preferred_element_type=F32)


def tn(a, b):
    return lax.dot_general(a, b, (((0,), (0,)), ((), ())), preferred_element_type=F32)


@functools.cache
def wave_lanes(waves):
    per = waves // SECTORS
    out = np.full((4, 256), -1, np.int64)
    for j in range(4):
        other = 4 if j == 0 else SECTORS - j
        out[j, :per] = SECTORS * np.arange(per) + j
        out[j, per : 2 * per] = SECTORS * np.arange(per) + other
    return out


@functools.cache
def dft_table(length, waves):
    sector = length // SECTORS
    per = waves // SECTORS
    lanes = wave_lanes(waves)
    t = np.arange(sector)
    table = np.zeros((4, 2, sector, 2, 256), np.float64)
    for j in range(4):
        m = lanes[j, : 2 * per]
        angle = 2.0 * math.pi * ((t[:, None] * m[None, :]) % length) / length
        c, s = np.cos(angle), np.sin(angle)
        if j == 0:
            table[j, 0, :, 0, :per] = c[:, :per]
            table[j, 0, :, 1, :per] = -s[:, :per]
            table[j, 1, :, 0, per : 2 * per] = c[:, per:]
            table[j, 1, :, 1, per : 2 * per] = -s[:, per:]
        else:
            sign = np.where(np.arange(2 * per) < per, 1.0, -1.0)
            table[j, 0, :, 0, : 2 * per] = c
            table[j, 0, :, 1, : 2 * per] = -s
            table[j, 1, :, 0, : 2 * per] = s * sign
            table[j, 1, :, 1, : 2 * per] = c * sign
    table = table.reshape(4, 2 * sector, 512) / math.sqrt(length)
    high = table.astype(ml_dtypes.bfloat16)
    low = (table - high.astype(np.float64)).astype(ml_dtypes.bfloat16)
    return high, low


@functools.cache
def order_table(waves):
    lanes = wave_lanes(waves).reshape(1024)
    return (np.arange(waves)[:, None] == lanes[None, :]).astype(ml_dtypes.bfloat16)


@functools.cache
def spread_table(cap):
    e = np.zeros((NZ, ROWS, 4, 128), np.float32)
    for z in range(NZ):
        for k in range(cap):
            for f in range(2):
                for r in range(2):
                    e[z, k * 4 + f * 2 + r, r * 2 + f, z * cap + k] = 1.0
    return e.reshape(NZ * ROWS, 512).astype(ml_dtypes.bfloat16)


@functools.cache
def lane_table():
    p = np.zeros((512, 512), np.float32)
    for z in range(4):
        for x in range(NX):
            for c in range(NC):
                for i in range(16):
                    lane = z * 32 + c * 16 + i
                    if x >= NX // 2:
                        lane = 127 - lane
                    p[z * 128 + (x * NC + c) * 16 + i, x * 128 + lane] = 1.0
    return p.astype(ml_dtypes.bfloat16)


def kernel(
    u_hbm, v_hbm, ws_hbm, cnt_hbm, visc_hbm, basis_hbm, hi_hbm, lo_hbm, e_hbm, pi_hbm, order_hbm,
    spec_ref, tend_ref,
    u_ref, v_ref, ws_ref, cnt_ref, visc_ref, order, basis, hi, lo, e_tab, pi_tab, onehot, damp,
    send_l, recv_l, send_a, recv_a, send_b, recv_b, turned,
    back_t, send_b2, recv_b2, send_a2, recv_a2, send_l2, recv_l2,
    load_sem, sl, rl, sa, ra, sb, rb, sb2, rb2, sa2, ra2, sl2, rl2,
):
    lat = lax.axis_index("lat")
    lon = lax.axis_index("lon")
    x = lat // (NZ * NC)
    z = lat // NC % NZ
    core = lat % NC
    group = x * NC + core
    cap, degrees, half_lat = basis.shape
    waves = ws_ref.shape[0]
    sector = u_ref.shape[2]

    def in_group(g):
        return (g // NC * (NZ * NC) + z * NC + g % NC, lon)

    def in_column(zz):
        return (lat + (zz - z) * NC, lon)

    def in_sector(s):
        return (lat, s)

    def partners(me, n):
        for d in sorted(range(1, n), key=lambda d: -min(d, n - d)):
            to = me + d
            yield jnp.where(to >= n, to - n, to)

    loads = [
        pltpu.make_async_copy(src, dst, load_sem.at[i])
        for i, (src, dst) in enumerate(
            (
                (u_hbm, u_ref), (v_hbm, v_ref), (ws_hbm, ws_ref), (cnt_hbm, cnt_ref), (visc_hbm, visc_ref),
                (order_hbm, order), (hi_hbm, hi), (lo_hbm, lo), (e_hbm, e_tab), (pi_hbm, pi_tab), (basis_hbm, basis),
            )
        )
    ]
    for load in loads:
        load.start()

    barrier = pltpu.get_barrier_semaphore()

    def greet(device_of, me, n):
        for to in partners(me, n):
            pl.semaphore_signal(barrier, inc=1, device_id=device_of(to), device_id_type=MESH)

    greet(in_sector, lon, SECTORS)
    greet(in_group, group, GROUPS)
    greet(in_column, z, NZ)

    loads[0].wait()
    loads[1].wait()

    def products(level, carry):
        u = u_ref[level]
        v = v_ref[level]
        send_l[level] = jnp.concatenate([u * v, u * u - v * v], axis=1)
        return carry

    lax.fori_loop(0, SECTORS, products, 0)
    recv_l[lon] = send_l[lon]
    pl.semaphore_wait(barrier, SECTORS + GROUPS + NZ - 3)

    def exchange(src, dst, send_sem, recv_sem, device_of, me, n):
        def start():
            for to in partners(me, n):
                pltpu.make_async_remote_copy(
                    src_ref=src.at[to],
                    dst_ref=dst.at[me],
                    send_sem=send_sem,
                    recv_sem=recv_sem,
                    device_id=device_of(to),
                    device_id_type=MESH,
                ).start()

        def landed():
            whole = dst.at[pl.ds(0, n - 1)]
            pltpu.make_async_copy(whole, whole, recv_sem).wait()

        def left():
            whole = src.at[pl.ds(0, n - 1)]
            pltpu.make_async_copy(whole, whole, send_sem).wait()

        return start, landed, left

    start, wait, left1 = exchange(send_l, recv_l, sl, rl, in_sector, lon, SECTORS)
    start()

    for load in loads[2:6]:
        load.wait()
    ws = ws_ref[...].reshape(1, waves)
    owner = ws // cap
    lane = (owner // (NZ * NC) * NC + owner % NC) * 128 + owner // NC % NZ * cap + ws % cap
    digit = lax.broadcasted_iota(jnp.int32, (16, waves), 0)
    digits = jnp.where(digit == 0, lane // 32, jnp.where(digit == 1, lane % 32, 1)).astype(F32)
    ordered = nn(digits.astype(BF16), order[...])
    target = (ordered[0:1] * 32.0 + ordered[1:2] + ordered[2:3] - 1.0).astype(jnp.int32)
    for b in range(GROUPS):
        ids = lax.broadcasted_iota(jnp.int32, (128, 1024), 0) + b * 128
        onehot[pl.ds(b * 128, 128), :] = jnp.where(ids == target, 1.0, 0.0).astype(BF16)

    rows40 = damp.shape[0]
    slot = lax.broadcasted_iota(jnp.int32, (rows40, waves), 0) // 4
    here = (ws == lat * cap + slot) & (slot < cap)
    wave_ids = lax.broadcasted_iota(jnp.int32, (rows40, waves), 1)
    wave_here = jnp.sum(jnp.where(here, wave_ids, 0).astype(F32), axis=1, keepdims=True)
    kept_here = jnp.sum(jnp.where(here, cnt_ref[...].reshape(1, waves), 0).astype(F32), axis=1, keepdims=True)
    levels = lax.broadcasted_iota(jnp.int32, (1, SECTORS), 1)
    rate = jnp.sum(jnp.where(levels == lon, visc_ref[...].reshape(1, SECTORS), 0.0), axis=1, keepdims=True)
    degree = lax.broadcasted_iota(jnp.int32, (rows40, degrees), 1).astype(F32)
    total = wave_here + degree
    q = total * (total + 1.0) / float(degrees * (degrees + 1))
    damping = (1.0 / math.sqrt(2 * half_lat)) / (1.0 + rate * (q * q))
    damp[...] = jnp.where(degree < kept_here, damping, 0.0)

    wait()
    loads[6].wait()
    loads[7].wait()

    a = [recv_l[s] for s in range(SECTORS)]
    e0, e1, e2, e3 = (a[i] + a[i + 4] for i in range(4))
    o0, o1, o2, o3 = (a[i] - a[i + 4] for i in range(4))
    od = HALF * (o1 - o3)
    os = HALF * (o1 + o3)
    sums = (
        (e0 + e1 + e2 + e3, e0 - e1 + e2 - e3),
        (o0 + od, -(os + o2)),
        (e0 - e2, e3 - e1),
        (o0 - od, o2 - os),
    )
    for j in range(4):
        one, two = sums[j]
        both = jnp.concatenate(
            [
                jnp.concatenate([one[:, :sector], two[:, :sector]], axis=1),
                jnp.concatenate([one[:, sector:], two[:, sector:]], axis=1),
            ],
            axis=0,
        )
        high = both.astype(BF16)
        low = (both - high.astype(F32)).astype(BF16)
        two = nn(jnp.concatenate([high, low], axis=0), hi[j])
        four = two[:32] + two[32:] + nn(high, lo[j])
        turned[0:32, pl.ds(j * 256, 256)] = four[:, :256].astype(BF16)
        turned[32:64, pl.ds(j * 256, 256)] = four[:, 256:].astype(BF16)

    placed = nt(turned[...], onehot[...]).astype(BF16)
    for g in range(GROUPS):
        for b in range(4):
            send_a[g, :, pl.ds(b * 128, 128)] = placed[b * 16 : b * 16 + 16, g * 128 : g * 128 + 128]
    start, wait, left2 = exchange(send_a, recv_a, sa, ra, in_group, group, GROUPS)
    start()
    recv_a[group] = send_a[group]
    loads[8].wait()
    wait()
    spread = nt(e_tab[...], recv_a[...].reshape(GROUPS * 16, 512)).astype(BF16)
    send_b[...] = spread.reshape(NZ, ROWS, 128)
    start, wait, left3 = exchange(send_b, recv_b, sb, rb, in_column, z, NZ)
    start()
    recv_b[z] = send_b[z]
    loads[9].wait()
    loads[10].wait()
    wait()

    quarters = NZ // 4
    gathered = jnp.concatenate(
        [
            jnp.concatenate([recv_b[4 * i + k] for k in range(4)], axis=1)
            for i in range(quarters)
        ],
        axis=0,
    )
    natural = nn(gathered, pi_tab[...])
    parity = jnp.where(lax.broadcasted_iota(jnp.int32, (8, degrees), 1) % 2 == 0, 1.0, -1.0)
    first = lax.broadcasted_iota(jnp.int32, (8, 1), 0) < 4
    blocks = half_lat // 128
    for i in range((cap + 1) // 2):
        r0 = 8 * i
        north, south = [], []
        for b in range(blocks):
            xx, gg = b // quarters, b % quarters
            north.append(natural[gg * ROWS + r0 : gg * ROWS + r0 + 8, xx * 128 : xx * 128 + 128])
            xx, gg = NX - 1 - xx, quarters - 1 - gg
            south.append(natural[gg * ROWS + r0 : gg * ROWS + r0 + 8, xx * 128 : xx * 128 + 128])
        both = jnp.concatenate(
            [jnp.concatenate(north, axis=1), jnp.concatenate(south, axis=1)], axis=0
        ).astype(BF16)
        raws = []
        for k in (2 * i, 2 * i + 1):
            if k < cap:
                out = nt(both, basis[k])
                raws.append(out[:8] + parity * out[8:])
        raw = jnp.where(first, raws[0], raws[1] if len(raws) > 1 else 0.0)
        spectral = raw * damp[pl.ds(r0, 8), :]
        for k in (2 * i, 2 * i + 1):
            if k < cap:
                at = 4 * (k - 2 * i)
                for f in range(2):
                    spec_ref[k, 0, f] = spectral[at + 2 * f : at + 2 * f + 2]
        rounded = spectral.astype(BF16).astype(F32)
        pair = jnp.concatenate([rounded, rounded * parity], axis=0).astype(BF16)
        outs = [nn(pair, basis[k]) for k in (2 * i, 2 * i + 1) if k < cap]
        keep = jnp.concatenate([first, first], axis=0)
        back = jnp.where(keep, outs[0], outs[1] if len(outs) > 1 else 0.0)
        back = back * (1.0 / math.sqrt(degrees))
        for b in range(blocks):
            xx, gg = b // quarters, b % quarters
            back_t[pl.ds(gg * ROWS + r0, 8), pl.ds(xx * 128, 128)] = back[:8, b * 128 : b * 128 + 128]
            xx, gg = NX - 1 - xx, quarters - 1 - gg
            back_t[pl.ds(gg * ROWS + r0, 8), pl.ds(xx * 128, 128)] = back[8:, b * 128 : b * 128 + 128]
    for gg in range(quarters):
        back_t[pl.ds(gg * ROWS + 40, 8), :] = jnp.zeros((8, 512), F32)

    mixed = nt(back_t[...].astype(BF16), pi_tab[...]).astype(BF16)
    for zz in range(NZ):
        send_b2[zz] = mixed[zz // 4 * ROWS : zz // 4 * ROWS + ROWS, zz % 4 * 128 : zz % 4 * 128 + 128]
    start, wait, left4 = exchange(send_b2, recv_b2, sb2, rb2, in_column, z, NZ)
    start()
    recv_b2[z] = send_b2[z]
    wait()
    joined = tn(recv_b2[...].reshape(NZ * ROWS, 128), e_tab[...]).astype(BF16)
    send_a2[...] = joined.reshape(GROUPS, 16, 512)
    start, wait, left5 = exchange(send_a2, recv_a2, sa2, ra2, in_group, group, GROUPS)
    start()
    recv_a2[group] = send_a2[group]
    wait()

    by_part = jnp.concatenate(
        [
            jnp.concatenate([recv_a2[g, :, pl.ds(b * 128, 128)] for g in range(GROUPS)], axis=1)
            for b in range(4)
        ],
        axis=0,
    )
    waved = nn(by_part, onehot[...])
    weight = jnp.where(lax.broadcasted_iota(jnp.int32, (1, 1024), 1) == 0, 1.0, 2.0)
    waved = (waved * weight).astype(BF16)
    parts = []
    for j in range(4):
        lhs = jnp.concatenate(
            [waved[:32, j * 256 : j * 256 + 256], waved[32:, j * 256 : j * 256 + 256]], axis=1
        )
        out = nt(lhs, hi[j]) + nt(lhs, lo[j])
        parts.append((out[:, :sector], out[:, sector:]))
    (u0, u4), (u1, v1), (u2, v2), (u3, v3) = parts
    even, odd = u0 + u4, u0 - u4
    ud, us = HALF * (u1 - u3), u1 + u3
    vd, vs = v1 - v3, HALF * (v1 + v3)
    grid = (
        even + us + u2,
        odd + ud - vs - v2,
        even - u2 - vd,
        odd - ud - vs + v2,
        even - us + u2,
        odd - ud + vs - v2,
        even - u2 + vd,
        odd + ud + vs + v2,
    )
    for s in range(SECTORS):
        send_l2[s] = jnp.concatenate([grid[s][:16], grid[s][16:]], axis=1).astype(BF16)
    start, wait, left6 = exchange(send_l2, recv_l2, sl2, rl2, in_sector, lon, SECTORS)
    start()
    recv_l2[lon] = send_l2[lon]
    wait()
    for s in range(SECTORS):
        both = recv_l2[s].astype(F32)
        tend_ref[s, 0] = both[:, :sector]
        tend_ref[s, 1] = both[:, sector:]
    for left in (left1, left2, left3, left4, left5, left6):
        left()


def body(wind_u, wind_v, basis, wave_slots, degree_count, viscosity):
    levels, lat_rows, sector = wind_u.shape
    cap, degrees, half_lat = basis.shape
    waves = wave_slots.shape[0]
    high, low = dft_table(sector * SECTORS, waves)
    vmem = pl.BlockSpec(memory_space=pltpu.VMEM)
    hbm = pl.BlockSpec(memory_space=pltpu.HBM)
    dma = pltpu.SemaphoreType.DMA
    return pl.pallas_call(
        kernel,
        out_shape=(
            jax.ShapeDtypeStruct((cap, 1, 2, 2, degrees), F32),
            jax.ShapeDtypeStruct((levels, 2, lat_rows, sector), F32),
        ),
        in_specs=[hbm] * 11,
        out_specs=(vmem, vmem),
        scratch_shapes=[
            pltpu.VMEM(wind_u.shape, F32),
            pltpu.VMEM(wind_v.shape, F32),
            pltpu.VMEM((waves,), jnp.int32),
            pltpu.VMEM((waves,), jnp.int32),
            pltpu.VMEM((levels,), F32),
            pltpu.VMEM((waves, 1024), BF16),
            pltpu.VMEM(basis.shape, BF16),
            pltpu.VMEM(high.shape, BF16),
            pltpu.VMEM(low.shape, BF16),
            pltpu.VMEM((NZ * ROWS, 512), BF16),
            pltpu.VMEM((512, 512), BF16),
            pltpu.VMEM((1024, 1024), BF16),
            pltpu.VMEM((40, degrees), F32),
            pltpu.VMEM((SECTORS, lat_rows, 2 * sector), F32),
            pltpu.VMEM((SECTORS, lat_rows, 2 * sector), F32),
            pltpu.VMEM((GROUPS, 16, 512), BF16),
            pltpu.VMEM((GROUPS, 16, 512), BF16),
            pltpu.VMEM((NZ, ROWS, 128), BF16),
            pltpu.VMEM((NZ, ROWS, 128), BF16),
            pltpu.VMEM((64, 1024), BF16),
            pltpu.VMEM((NZ // 4 * ROWS, 512), F32),
            pltpu.VMEM((NZ, ROWS, 128), BF16),
            pltpu.VMEM((NZ, ROWS, 128), BF16),
            pltpu.VMEM((GROUPS, 16, 512), BF16),
            pltpu.VMEM((GROUPS, 16, 512), BF16),
            pltpu.VMEM((SECTORS, lat_rows, 2 * sector), BF16),
            pltpu.VMEM((SECTORS, lat_rows, 2 * sector), BF16),
            dma((11,)),
        ]
        + [dma(())] * 12,
        compiler_params=pltpu.CompilerParams(
            collective_id=0, has_side_effects=True, vmem_limit_bytes=40 * 2**20
        ),
    )(
        *(
            pltpu.with_memory_space_constraint(operand, pltpu.HBM)
            for operand in (
                wind_u,
                wind_v,
                wave_slots,
                degree_count,
                viscosity,
                basis,
                jnp.asarray(high),
                jnp.asarray(low),
                jnp.asarray(spread_table(cap)),
                jnp.asarray(lane_table()),
                jnp.asarray(order_table(waves)),
            )
        )
    )


def solution(mesh):
    return jax.shard_map(
        body,
        mesh=mesh,
        in_specs=(
            P(None, "lat", "lon"),
            P(None, "lat", "lon"),
            P("lat", None, None),
            P(),
            P(),
            P(),
        ),
        out_specs=(P("lat", "lon", None, None, None), P(None, None, "lat", "lon")),
        check_vma=False,
    )
```

```python
import functools
import math

import jax
import jax.numpy as jnp
import ml_dtypes
import numpy as np
from jax import lax
from jax.experimental import pallas as pl
from jax.experimental.pallas import tpu as pltpu
from jax.sharding import PartitionSpec as P

MESH = pl.DeviceIdType.MESH
F32 = jnp.float32
BF16 = jnp.bfloat16

NX, NZ, NC = 4, 12, 2
GROUPS = NX * NC
SECTORS = 8
PARTS = 3
ROWS = 16
HALF = math.sqrt(0.5)


def nt(a, b):
    return lax.dot_general(a, b, (((1,), (1,)), ((), ())), preferred_element_type=F32)


def nn(a, b):
    return lax.dot_general(a, b, (((1,), (0,)), ((), ())), preferred_element_type=F32)


def tn(a, b):
    return lax.dot_general(a, b, (((0,), (0,)), ((), ())), preferred_element_type=F32)


@functools.cache
def wave_lanes(waves):
    per = waves // SECTORS
    out = np.full((4, 256), -1, np.int64)
    for j in range(4):
        other = 4 if j == 0 else SECTORS - j
        out[j, :per] = SECTORS * np.arange(per) + j
        out[j, per : 2 * per] = SECTORS * np.arange(per) + other
    return out


@functools.cache
def dft_table(length, waves):
    sector = length // SECTORS
    per = waves // SECTORS
    lanes = wave_lanes(waves)
    t = np.arange(sector)
    table = np.zeros((4, 2, sector, 2, 256), np.float64)
    for j in range(4):
        m = lanes[j, : 2 * per]
        angle = 2.0 * math.pi * ((t[:, None] * m[None, :]) % length) / length
        c, s = np.cos(angle), np.sin(angle)
        if j == 0:
            table[j, 0, :, 0, :per] = c[:, :per]
            table[j, 0, :, 1, :per] = -s[:, :per]
            table[j, 1, :, 0, per : 2 * per] = c[:, per:]
            table[j, 1, :, 1, per : 2 * per] = -s[:, per:]
        else:
            sign = np.where(np.arange(2 * per) < per, 1.0, -1.0)
            table[j, 0, :, 0, : 2 * per] = c
            table[j, 0, :, 1, : 2 * per] = -s
            table[j, 1, :, 0, : 2 * per] = s * sign
            table[j, 1, :, 1, : 2 * per] = c * sign
    table = table.reshape(4, 2 * sector, 512) / math.sqrt(length)
    high = table.astype(ml_dtypes.bfloat16)
    low = (table - high.astype(np.float64)).astype(ml_dtypes.bfloat16)
    return high, low


@functools.cache
def order_table(waves):
    lanes = wave_lanes(waves).reshape(1024)
    return (np.arange(waves)[:, None] == lanes[None, :]).astype(ml_dtypes.bfloat16)


@functools.cache
def spread_table(cap):
    e = np.zeros((PARTS, NZ, ROWS, 4, 128), np.float32)
    for z in range(NZ):
        for k in range(cap):
            for f in range(2):
                for r in range(2):
                    e[k // 4, z, k % 4 * 4 + f * 2 + r, r * 2 + f, z * cap + k] = 1.0
    return e.reshape(PARTS * NZ * ROWS, 512).astype(ml_dtypes.bfloat16)


@functools.cache
def lane_table():
    p = np.zeros((512, 512), np.float32)
    for z in range(4):
        for x in range(NX):
            for c in range(NC):
                for i in range(16):
                    lane = z * 32 + c * 16 + i
                    if x >= NX // 2:
                        lane = 127 - lane
                    p[z * 128 + (x * NC + c) * 16 + i, x * 128 + lane] = 1.0
    return p.astype(ml_dtypes.bfloat16)


def kernel(
    u_hbm, v_hbm, ws_hbm, cnt_hbm, visc_hbm, basis_hbm, hi_hbm, lo_hbm, e_hbm, pi_hbm, order_hbm,
    spec_ref, tend_ref,
    u_ref, v_ref, ws_ref, cnt_ref, visc_ref, order, basis, hi, lo, e_tab, pi_tab, onehot, damp,
    send_l, recv_l, send_a, recv_a, send_b, recv_b, turned,
    back_t, send_b2, recv_b2, send_a2, recv_a2, send_l2, recv_l2,
    load_sem, sl, rl, sa, ra, sb, rb, sb2, rb2, sa2, ra2, sl2, rl2,
):
    lat = lax.axis_index("lat")
    lon = lax.axis_index("lon")
    x = lat // (NZ * NC)
    z = lat // NC % NZ
    core = lat % NC
    group = x * NC + core
    cap, degrees, half_lat = basis.shape
    waves = ws_ref.shape[0]
    sector = u_ref.shape[2]

    def in_group(g):
        return (g // NC * (NZ * NC) + z * NC + g % NC, lon)

    def in_column(zz):
        return (lat + (zz - z) * NC, lon)

    def in_sector(s):
        return (lat, s)

    def partners(me, n):
        for d in sorted(range(1, n), key=lambda d: -min(d, n - d)):
            to = me + d
            yield jnp.where(to >= n, to - n, to)

    loads = [
        pltpu.make_async_copy(src, dst, load_sem.at[i])
        for i, (src, dst) in enumerate(
            (
                (u_hbm, u_ref), (v_hbm, v_ref), (ws_hbm, ws_ref), (cnt_hbm, cnt_ref), (visc_hbm, visc_ref),
                (order_hbm, order), (hi_hbm, hi), (lo_hbm, lo), (e_hbm, e_tab), (pi_hbm, pi_tab), (basis_hbm, basis),
            )
        )
    ]
    for load in loads[:2]:
        load.start()

    barrier = pltpu.get_barrier_semaphore()

    def greet(device_of, me, n):
        for to in partners(me, n):
            pl.semaphore_signal(barrier, inc=1, device_id=device_of(to), device_id_type=MESH)

    greet(in_sector, lon, SECTORS)
    greet(in_group, group, GROUPS)
    greet(in_column, z, NZ)

    for load in loads[2:]:
        load.start()
    loads[0].wait()
    loads[1].wait()

    pl.semaphore_wait(barrier, SECTORS + GROUPS + NZ - 3)

    def exchange(src, dst, send_sem, recv_sem, device_of, me, n):
        def start(prepare=None):
            for to in partners(me, n):
                if prepare is not None:
                    prepare(to)
                pltpu.make_async_remote_copy(
                    src_ref=src.at[to],
                    dst_ref=dst.at[me],
                    send_sem=send_sem,
                    recv_sem=recv_sem,
                    device_id=device_of(to),
                    device_id_type=MESH,
                ).start()

        def landed():
            whole = dst.at[pl.ds(0, n - 1)]
            pltpu.make_async_copy(whole, whole, recv_sem).wait()

        def left():
            whole = src.at[pl.ds(0, n - 1)]
            pltpu.make_async_copy(whole, whole, send_sem).wait()

        return start, landed, left

    def products(level):
        u = u_ref[level]
        v = v_ref[level]
        return jnp.concatenate([u * v, u * u - v * v], axis=1)

    def prepare(level):
        send_l[level] = products(level)

    start, wait, left1 = exchange(send_l, recv_l, sl, rl, in_sector, lon, SECTORS)
    start(prepare)
    recv_l[lon] = products(lon)

    for load in loads[2:6]:
        load.wait()
    ws = ws_ref[...].reshape(1, waves)
    owner = ws // cap
    lane = (owner // (NZ * NC) * NC + owner % NC) * 128 + owner // NC % NZ * cap + ws % cap
    digit = lax.broadcasted_iota(jnp.int32, (16, waves), 0)
    digits = jnp.where(digit == 0, lane // 32, jnp.where(digit == 1, lane % 32, 1)).astype(F32)
    ordered = nn(digits.astype(BF16), order[...])
    target = (ordered[0:1] * 32.0 + ordered[1:2] + ordered[2:3] - 1.0).astype(jnp.int32)
    for b in range(GROUPS):
        ids = lax.broadcasted_iota(jnp.int32, (128, 1024), 0) + b * 128
        onehot[pl.ds(b * 128, 128), :] = jnp.where(ids == target, 1.0, 0.0).astype(BF16)

    rows40 = damp.shape[0]
    slot = lax.broadcasted_iota(jnp.int32, (rows40, waves), 0) // 4
    here = (ws == lat * cap + slot) & (slot < cap)
    wave_ids = lax.broadcasted_iota(jnp.int32, (rows40, waves), 1)
    wave_here = jnp.sum(jnp.where(here, wave_ids, 0).astype(F32), axis=1, keepdims=True)
    kept_here = jnp.sum(jnp.where(here, cnt_ref[...].reshape(1, waves), 0).astype(F32), axis=1, keepdims=True)
    levels = lax.broadcasted_iota(jnp.int32, (1, SECTORS), 1)
    rate = jnp.sum(jnp.where(levels == lon, visc_ref[...].reshape(1, SECTORS), 0.0), axis=1, keepdims=True)
    degree = lax.broadcasted_iota(jnp.int32, (rows40, degrees), 1).astype(F32)
    total = wave_here + degree
    q = total * (total + 1.0) / float(degrees * (degrees + 1))
    damping = (1.0 / math.sqrt(2 * half_lat)) / (1.0 + rate * (q * q))
    damp[...] = jnp.where(degree < kept_here, damping, 0.0)

    wait()
    loads[6].wait()
    loads[7].wait()

    a = [recv_l[s] for s in range(SECTORS)]
    e0, e1, e2, e3 = (a[i] + a[i + 4] for i in range(4))
    o0, o1, o2, o3 = (a[i] - a[i + 4] for i in range(4))
    od = HALF * (o1 - o3)
    os = HALF * (o1 + o3)
    sums = (
        (e0 + e1 + e2 + e3, e0 - e1 + e2 - e3),
        (o0 + od, -(os + o2)),
        (e0 - e2, e3 - e1),
        (o0 - od, o2 - os),
    )
    for j in range(4):
        one, two = sums[j]
        both = jnp.concatenate(
            [
                jnp.concatenate([one[:, :sector], two[:, :sector]], axis=1),
                jnp.concatenate([one[:, sector:], two[:, sector:]], axis=1),
            ],
            axis=0,
        )
        high = both.astype(BF16)
        low = (both - high.astype(F32)).astype(BF16)
        two = nn(jnp.concatenate([high, low], axis=0), hi[j])
        four = two[:32] + two[32:] + nn(high, lo[j])
        turned[0:32, pl.ds(j * 256, 256)] = four[:, :256].astype(BF16)
        turned[32:64, pl.ds(j * 256, 256)] = four[:, 256:].astype(BF16)

    placed = nt(turned[...], onehot[...]).astype(BF16)
    for g in range(GROUPS):
        for b in range(4):
            send_a[g, :, pl.ds(b * 128, 128)] = placed[b * 16 : b * 16 + 16, g * 128 : g * 128 + 128]
    start, wait, left2 = exchange(send_a, recv_a, sa, ra, in_group, group, GROUPS)
    start()
    recv_a[group] = send_a[group]
    loads[8].wait()
    wait()
    spread = nt(e_tab[...], recv_a[...].reshape(GROUPS * 16, 512)).astype(BF16)
    send_b[...] = spread.reshape(PARTS, NZ, ROWS, 128)
    there = [
        exchange(send_b.at[p], recv_b.at[p], sb.at[p], rb.at[p], in_column, z, NZ) for p in range(PARTS)
    ]
    back = [
        exchange(send_b2.at[p], recv_b2.at[p], sb2.at[p], rb2.at[p], in_column, z, NZ)
        for p in range(PARTS)
    ]
    for p in range(PARTS):
        there[p][0]()
    for p in range(PARTS):
        recv_b[p, z] = send_b[p, z]
    loads[9].wait()
    loads[10].wait()

    quarters = NZ // 4
    parity = jnp.where(lax.broadcasted_iota(jnp.int32, (8, degrees), 1) % 2 == 0, 1.0, -1.0)
    first = lax.broadcasted_iota(jnp.int32, (8, 1), 0) < 4
    blocks = half_lat // 128
    for p in range(PARTS):
        there[p][1]()
        gathered = jnp.concatenate(
            [
                jnp.concatenate([recv_b[p, 4 * i + k] for k in range(4)], axis=1)
                for i in range(quarters)
            ],
            axis=0,
        )
        natural = nn(gathered, pi_tab[...])
        for i in range(2 * p, min(2 * p + 2, (cap + 1) // 2)):
            r0 = 8 * (i - 2 * p)
            north, south = [], []
            for b in range(blocks):
                xx, gg = b // quarters, b % quarters
                north.append(natural[gg * ROWS + r0 : gg * ROWS + r0 + 8, xx * 128 : xx * 128 + 128])
                xx, gg = NX - 1 - xx, quarters - 1 - gg
                south.append(natural[gg * ROWS + r0 : gg * ROWS + r0 + 8, xx * 128 : xx * 128 + 128])
            both = jnp.concatenate(
                [jnp.concatenate(north, axis=1), jnp.concatenate(south, axis=1)], axis=0
            ).astype(BF16)
            raws = []
            for k in (2 * i, 2 * i + 1):
                if k < cap:
                    out = nt(both, basis[k])
                    raws.append(out[:8] + parity * out[8:])
            raw = jnp.where(first, raws[0], raws[1] if len(raws) > 1 else 0.0)
            spectral = raw * damp[pl.ds(8 * i, 8), :]
            for k in (2 * i, 2 * i + 1):
                if k < cap:
                    at = 4 * (k - 2 * i)
                    for f in range(2):
                        spec_ref[k, 0, f] = spectral[at + 2 * f : at + 2 * f + 2]
            rounded = spectral.astype(BF16).astype(F32)
            pair = jnp.concatenate([rounded, rounded * parity], axis=0).astype(BF16)
            outs = [nn(pair, basis[k]) for k in (2 * i, 2 * i + 1) if k < cap]
            keep = jnp.concatenate([first, first], axis=0)
            synth = jnp.where(keep, outs[0], outs[1] if len(outs) > 1 else 0.0)
            synth = synth * (1.0 / math.sqrt(degrees))
            for b in range(blocks):
                xx, gg = b // quarters, b % quarters
                back_t[p, pl.ds(gg * ROWS + r0, 8), pl.ds(xx * 128, 128)] = synth[:8, b * 128 : b * 128 + 128]
                xx, gg = NX - 1 - xx, quarters - 1 - gg
                back_t[p, pl.ds(gg * ROWS + r0, 8), pl.ds(xx * 128, 128)] = synth[8:, b * 128 : b * 128 + 128]
        for gg in range(quarters):
            if 2 * p + 2 > (cap + 1) // 2:
                back_t[p, pl.ds(gg * ROWS + 8, 8), :] = jnp.zeros((8, 512), F32)
        mixed = nt(back_t[p].astype(BF16), pi_tab[...]).astype(BF16)
        for zz in range(NZ):
            send_b2[p, zz] = mixed[zz // 4 * ROWS : zz // 4 * ROWS + ROWS, zz % 4 * 128 : zz % 4 * 128 + 128]
        back[p][0]()
        recv_b2[p, z] = send_b2[p, z]

    joined = 0.0
    for p in range(PARTS):
        back[p][1]()
        rows = NZ * ROWS
        joined += tn(recv_b2[p].reshape(rows, 128), e_tab[pl.ds(p * rows, rows), :])
    send_a2[...] = joined.astype(BF16).reshape(GROUPS, 16, 512)
    start, wait, left5 = exchange(send_a2, recv_a2, sa2, ra2, in_group, group, GROUPS)
    start()
    recv_a2[group] = send_a2[group]
    wait()

    by_part = jnp.concatenate(
        [
            jnp.concatenate([recv_a2[g, :, pl.ds(b * 128, 128)] for g in range(GROUPS)], axis=1)
            for b in range(4)
        ],
        axis=0,
    )
    waved = nn(by_part, onehot[...])
    weight = jnp.where(lax.broadcasted_iota(jnp.int32, (1, 1024), 1) == 0, 1.0, 2.0)
    waved = (waved * weight).astype(BF16)
    parts = []
    for j in range(4):
        lhs = jnp.concatenate(
            [waved[:32, j * 256 : j * 256 + 256], waved[32:, j * 256 : j * 256 + 256]], axis=1
        )
        out = nt(lhs, hi[j]) + nt(lhs, lo[j])
        parts.append((out[:, :sector], out[:, sector:]))
    (u0, u4), (u1, v1), (u2, v2), (u3, v3) = parts
    even, odd = u0 + u4, u0 - u4
    ud, us = HALF * (u1 - u3), u1 + u3
    vd, vs = v1 - v3, HALF * (v1 + v3)
    grid = (
        even + us + u2,
        odd + ud - vs - v2,
        even - u2 - vd,
        odd - ud - vs + v2,
        even - us + u2,
        odd - ud + vs - v2,
        even - u2 + vd,
        odd + ud + vs + v2,
    )
    for s in range(SECTORS):
        send_l2[s] = jnp.concatenate([grid[s][:16], grid[s][16:]], axis=1).astype(BF16)
    start, wait, left6 = exchange(send_l2, recv_l2, sl2, rl2, in_sector, lon, SECTORS)
    start()
    recv_l2[lon] = send_l2[lon]
    wait()
    for s in range(SECTORS):
        both = recv_l2[s].astype(F32)
        tend_ref[s, 0] = both[:, :sector]
        tend_ref[s, 1] = both[:, sector:]
    for left in (left1, left2, left5, left6, *(e[2] for e in there), *(e[2] for e in back)):
        left()


def body(wind_u, wind_v, basis, wave_slots, degree_count, viscosity):
    levels, lat_rows, sector = wind_u.shape
    cap, degrees, half_lat = basis.shape
    waves = wave_slots.shape[0]
    high, low = dft_table(sector * SECTORS, waves)
    vmem = pl.BlockSpec(memory_space=pltpu.VMEM)
    hbm = pl.BlockSpec(memory_space=pltpu.HBM)
    dma = pltpu.SemaphoreType.DMA
    return pl.pallas_call(
        kernel,
        out_shape=(
            jax.ShapeDtypeStruct((cap, 1, 2, 2, degrees), F32),
            jax.ShapeDtypeStruct((levels, 2, lat_rows, sector), F32),
        ),
        in_specs=[hbm] * 11,
        out_specs=(vmem, vmem),
        scratch_shapes=[
            pltpu.VMEM(wind_u.shape, F32),
            pltpu.VMEM(wind_v.shape, F32),
            pltpu.VMEM((waves,), jnp.int32),
            pltpu.VMEM((waves,), jnp.int32),
            pltpu.VMEM((levels,), F32),
            pltpu.VMEM((waves, 1024), BF16),
            pltpu.VMEM(basis.shape, BF16),
            pltpu.VMEM(high.shape, BF16),
            pltpu.VMEM(low.shape, BF16),
            pltpu.VMEM((PARTS * NZ * ROWS, 512), BF16),
            pltpu.VMEM((512, 512), BF16),
            pltpu.VMEM((1024, 1024), BF16),
            pltpu.VMEM((40, degrees), F32),
            pltpu.VMEM((SECTORS, lat_rows, 2 * sector), F32),
            pltpu.VMEM((SECTORS, lat_rows, 2 * sector), F32),
            pltpu.VMEM((GROUPS, 16, 512), BF16),
            pltpu.VMEM((GROUPS, 16, 512), BF16),
            pltpu.VMEM((PARTS, NZ, ROWS, 128), BF16),
            pltpu.VMEM((PARTS, NZ, ROWS, 128), BF16),
            pltpu.VMEM((64, 1024), BF16),
            pltpu.VMEM((PARTS, NZ // 4 * ROWS, 512), F32),
            pltpu.VMEM((PARTS, NZ, ROWS, 128), BF16),
            pltpu.VMEM((PARTS, NZ, ROWS, 128), BF16),
            pltpu.VMEM((GROUPS, 16, 512), BF16),
            pltpu.VMEM((GROUPS, 16, 512), BF16),
            pltpu.VMEM((SECTORS, lat_rows, 2 * sector), BF16),
            pltpu.VMEM((SECTORS, lat_rows, 2 * sector), BF16),
            dma((11,)),
        ]
        + [dma(())] * 4 + [dma((PARTS,))] * 4 + [dma(())] * 4,
        compiler_params=pltpu.CompilerParams(
            collective_id=0, has_side_effects=True, vmem_limit_bytes=40 * 2**20
        ),
    )(
        *(
            pltpu.with_memory_space_constraint(operand, pltpu.HBM)
            for operand in (
                wind_u,
                wind_v,
                wave_slots,
                degree_count,
                viscosity,
                basis,
                jnp.asarray(high),
                jnp.asarray(low),
                jnp.asarray(spread_table(cap)),
                jnp.asarray(lane_table()),
                jnp.asarray(order_table(waves)),
            )
        )
    )


def solution(mesh):
    return jax.shard_map(
        body,
        mesh=mesh,
        in_specs=(
            P(None, "lat", "lon"),
            P(None, "lat", "lon"),
            P("lat", None, None),
            P(),
            P(),
            P(),
        ),
        out_specs=(P("lat", "lon", None, None, None), P(None, None, "lat", "lon")),
        check_vma=False,
    )
```

```python
import functools
import math

import jax
import jax.numpy as jnp
import ml_dtypes
import numpy as np
from jax import lax
from jax.experimental import pallas as pl
from jax.experimental.pallas import tpu as pltpu
from jax.sharding import PartitionSpec as P

MESH = pl.DeviceIdType.MESH
F32 = jnp.float32
BF16 = jnp.bfloat16

NX, NZ, NC = 4, 12, 2
GROUPS = NX * NC
SECTORS = 8
PARTS = 2
ROWS = 16
REST = 4
HALF = math.sqrt(0.5)


def nt(a, b):
    return lax.dot_general(a, b, (((1,), (1,)), ((), ())), preferred_element_type=F32)


def nn(a, b):
    return lax.dot_general(a, b, (((1,), (0,)), ((), ())), preferred_element_type=F32)


def tn(a, b):
    return lax.dot_general(a, b, (((0,), (0,)), ((), ())), preferred_element_type=F32)


@functools.cache
def wave_lanes(waves):
    per = waves // SECTORS
    out = np.full((4, 256), -1, np.int64)
    for j in range(4):
        other = 4 if j == 0 else SECTORS - j
        out[j, :per] = SECTORS * np.arange(per) + j
        out[j, per : 2 * per] = SECTORS * np.arange(per) + other
    return out


@functools.cache
def dft_table(length, waves):
    sector = length // SECTORS
    per = waves // SECTORS
    lanes = wave_lanes(waves)
    t = np.arange(sector)
    table = np.zeros((4, 2, sector, 2, 256), np.float64)
    for j in range(4):
        m = lanes[j, : 2 * per]
        angle = 2.0 * math.pi * ((t[:, None] * m[None, :]) % length) / length
        c, s = np.cos(angle), np.sin(angle)
        if j == 0:
            table[j, 0, :, 0, :per] = c[:, :per]
            table[j, 0, :, 1, :per] = -s[:, :per]
            table[j, 1, :, 0, per : 2 * per] = c[:, per:]
            table[j, 1, :, 1, per : 2 * per] = -s[:, per:]
        else:
            sign = np.where(np.arange(2 * per) < per, 1.0, -1.0)
            table[j, 0, :, 0, : 2 * per] = c
            table[j, 0, :, 1, : 2 * per] = -s
            table[j, 1, :, 0, : 2 * per] = s * sign
            table[j, 1, :, 1, : 2 * per] = c * sign
    table = table.reshape(4, 2 * sector, 512) / math.sqrt(length)
    high = table.astype(ml_dtypes.bfloat16)
    low = (table - high.astype(np.float64)).astype(ml_dtypes.bfloat16)
    return high, low


@functools.cache
def order_table(waves):
    lanes = wave_lanes(waves).reshape(1024)
    return (np.arange(waves)[:, None] == lanes[None, :]).astype(ml_dtypes.bfloat16)


@functools.cache
def spread_table(cap):
    e = np.zeros((PARTS, NZ, ROWS, 4, 128), np.float32)
    rest = np.zeros((NZ, REST, 4, 128), np.float32)
    for z in range(NZ):
        for k in range(cap):
            for f in range(2):
                for r in range(2):
                    rows = e[k // 4] if k < 4 * PARTS else rest
                    rows[z, k % 4 * 4 + f * 2 + r, r * 2 + f, z * cap + k] = 1.0
    both = np.concatenate([e.reshape(PARTS * NZ * ROWS, 512), rest.reshape(NZ * REST, 512)])
    return both.astype(ml_dtypes.bfloat16)


@functools.cache
def lane_table():
    p = np.zeros((512, 512), np.float32)
    for z in range(4):
        for x in range(NX):
            for c in range(NC):
                for i in range(16):
                    lane = z * 32 + c * 16 + i
                    if x >= NX // 2:
                        lane = 127 - lane
                    p[z * 128 + (x * NC + c) * 16 + i, x * 128 + lane] = 1.0
    return p.astype(ml_dtypes.bfloat16)


def kernel(
    u_hbm, v_hbm, ws_hbm, cnt_hbm, visc_hbm, basis_hbm, hi_hbm, lo_hbm, e_hbm, pi_hbm, order_hbm,
    spec_ref, tend_ref,
    u_ref, v_ref, ws_ref, cnt_ref, visc_ref, order, basis, hi, lo, e_tab, pi_tab, onehot, damp,
    send_l, recv_l, send_a, recv_a, send_b, recv_b, turned,
    back_t, send_b2, recv_b2, send_c, recv_c, send_c2, recv_c2, send_a2, recv_a2, send_l2, recv_l2,
    load_sem, sl, rl, sa, ra, sb, rb, sb2, rb2, sa2, ra2, sl2, rl2,
):
    lat = lax.axis_index("lat")
    lon = lax.axis_index("lon")
    x = lat // (NZ * NC)
    z = lat // NC % NZ
    core = lat % NC
    group = x * NC + core
    cap, degrees, half_lat = basis.shape
    waves = ws_ref.shape[0]
    sector = u_ref.shape[2]

    def in_group(g):
        return (g // NC * (NZ * NC) + z * NC + g % NC, lon)

    def in_column(zz):
        return (lat + (zz - z) * NC, lon)

    def in_sector(s):
        return (lat, s)

    def partners(me, n):
        for d in sorted(range(1, n), key=lambda d: -min(d, n - d)):
            to = me + d
            yield jnp.where(to >= n, to - n, to)

    loads = [
        pltpu.make_async_copy(src, dst, load_sem.at[i])
        for i, (src, dst) in enumerate(
            (
                (u_hbm, u_ref), (v_hbm, v_ref), (ws_hbm, ws_ref), (cnt_hbm, cnt_ref), (visc_hbm, visc_ref),
                (order_hbm, order), (hi_hbm, hi), (lo_hbm, lo), (e_hbm, e_tab), (pi_hbm, pi_tab), (basis_hbm, basis),
            )
        )
    ]
    for load in loads[:2]:
        load.start()

    barrier = pltpu.get_barrier_semaphore()

    def greet(device_of, me, n):
        for to in partners(me, n):
            pl.semaphore_signal(barrier, inc=1, device_id=device_of(to), device_id_type=MESH)

    greet(in_sector, lon, SECTORS)
    greet(in_group, group, GROUPS)
    greet(in_column, z, NZ)

    for load in loads[2:]:
        load.start()
    loads[0].wait()
    loads[1].wait()

    pl.semaphore_wait(barrier, SECTORS + GROUPS + NZ - 3)

    def exchange(src, dst, send_sem, recv_sem, device_of, me, n):
        def start(prepare=None):
            for to in partners(me, n):
                if prepare is not None:
                    prepare(to)
                pltpu.make_async_remote_copy(
                    src_ref=src.at[to],
                    dst_ref=dst.at[me],
                    send_sem=send_sem,
                    recv_sem=recv_sem,
                    device_id=device_of(to),
                    device_id_type=MESH,
                ).start()

        def landed():
            whole = dst.at[pl.ds(0, n - 1)]
            pltpu.make_async_copy(whole, whole, recv_sem).wait()

        def left():
            whole = src.at[pl.ds(0, n - 1)]
            pltpu.make_async_copy(whole, whole, send_sem).wait()

        return start, landed, left

    def products(level):
        u = u_ref[level]
        v = v_ref[level]
        return jnp.concatenate([u * v, u * u - v * v], axis=1)

    def prepare(level):
        send_l[level] = products(level)

    start, wait, left1 = exchange(send_l, recv_l, sl, rl, in_sector, lon, SECTORS)
    start(prepare)
    recv_l[lon] = products(lon)

    for load in loads[2:6]:
        load.wait()
    ws = ws_ref[...].reshape(1, waves)
    owner = ws // cap
    lane = (owner // (NZ * NC) * NC + owner % NC) * 128 + owner // NC % NZ * cap + ws % cap
    digit = lax.broadcasted_iota(jnp.int32, (16, waves), 0)
    digits = jnp.where(digit == 0, lane // 32, jnp.where(digit == 1, lane % 32, 1)).astype(F32)
    ordered = nn(digits.astype(BF16), order[...])
    target = (ordered[0:1] * 32.0 + ordered[1:2] + ordered[2:3] - 1.0).astype(jnp.int32)
    for b in range(GROUPS):
        ids = lax.broadcasted_iota(jnp.int32, (128, 1024), 0) + b * 128
        onehot[pl.ds(b * 128, 128), :] = jnp.where(ids == target, 1.0, 0.0).astype(BF16)

    rows40 = damp.shape[0]
    slot = lax.broadcasted_iota(jnp.int32, (rows40, waves), 0) // 4
    here = (ws == lat * cap + slot) & (slot < cap)
    wave_ids = lax.broadcasted_iota(jnp.int32, (rows40, waves), 1)
    wave_here = jnp.sum(jnp.where(here, wave_ids, 0).astype(F32), axis=1, keepdims=True)
    kept_here = jnp.sum(jnp.where(here, cnt_ref[...].reshape(1, waves), 0).astype(F32), axis=1, keepdims=True)
    levels = lax.broadcasted_iota(jnp.int32, (1, SECTORS), 1)
    rate = jnp.sum(jnp.where(levels == lon, visc_ref[...].reshape(1, SECTORS), 0.0), axis=1, keepdims=True)
    degree = lax.broadcasted_iota(jnp.int32, (rows40, degrees), 1).astype(F32)
    total = wave_here + degree
    q = total * (total + 1.0) / float(degrees * (degrees + 1))
    damping = (1.0 / math.sqrt(2 * half_lat)) / (1.0 + rate * (q * q))
    damp[...] = jnp.where(degree < kept_here, damping, 0.0)

    wait()
    loads[6].wait()
    loads[7].wait()

    a = [recv_l[s] for s in range(SECTORS)]
    e0, e1, e2, e3 = (a[i] + a[i + 4] for i in range(4))
    o0, o1, o2, o3 = (a[i] - a[i + 4] for i in range(4))
    od = HALF * (o1 - o3)
    os = HALF * (o1 + o3)
    sums = (
        (e0 + e1 + e2 + e3, e0 - e1 + e2 - e3),
        (o0 + od, -(os + o2)),
        (e0 - e2, e3 - e1),
        (o0 - od, o2 - os),
    )
    for j in range(4):
        one, two = sums[j]
        both = jnp.concatenate(
            [
                jnp.concatenate([one[:, :sector], two[:, :sector]], axis=1),
                jnp.concatenate([one[:, sector:], two[:, sector:]], axis=1),
            ],
            axis=0,
        )
        high = both.astype(BF16)
        low = (both - high.astype(F32)).astype(BF16)
        two = nn(jnp.concatenate([high, low], axis=0), hi[j])
        four = two[:32] + two[32:] + nn(high, lo[j])
        turned[0:32, pl.ds(j * 256, 256)] = four[:, :256].astype(BF16)
        turned[32:64, pl.ds(j * 256, 256)] = four[:, 256:].astype(BF16)

    placed = nt(turned[...], onehot[...]).astype(BF16)
    for g in range(GROUPS):
        for b in range(4):
            send_a[g, :, pl.ds(b * 128, 128)] = placed[b * 16 : b * 16 + 16, g * 128 : g * 128 + 128]
    start, wait, left2 = exchange(send_a, recv_a, sa, ra, in_group, group, GROUPS)
    start()
    recv_a[group] = send_a[group]
    loads[8].wait()
    wait()
    spread = nt(e_tab[...], recv_a[...].reshape(GROUPS * 16, 512))
    full = PARTS * NZ * ROWS
    send_b[...] = spread[:full].astype(BF16).reshape(PARTS, NZ, ROWS, 128)
    for zz in range(NZ):
        send_c[zz] = spread[full + REST * zz : full + REST * zz + REST]

    def over_z(src, dst, send_sems, recv_sems, rest_src, rest_dst):
        pieces = [(src.at[p], dst.at[p]) for p in range(PARTS)] + [(rest_src, rest_dst)]
        return [
            exchange(a, b, send_sems.at[p], recv_sems.at[p], in_column, z, NZ)
            for p, (a, b) in enumerate(pieces)
        ]

    there = over_z(send_b, recv_b, sb, rb, send_c, recv_c)
    back = over_z(send_b2, recv_b2, sb2, rb2, send_c2, recv_c2)
    for p in range(PARTS + 1):
        there[p][0]()
    for p in range(PARTS):
        recv_b[p, z] = send_b[p, z]
    recv_c[z] = send_c[z]
    loads[9].wait()
    loads[10].wait()

    quarters = NZ // 4
    parity = jnp.where(lax.broadcasted_iota(jnp.int32, (8, degrees), 1) % 2 == 0, 1.0, -1.0)
    first = lax.broadcasted_iota(jnp.int32, (8, 1), 0) < 4
    blocks = half_lat // 128
    pad = jnp.zeros((ROWS - REST, 512), F32)
    for p in range(PARTS + 1):
        there[p][1]()
        gathered = []
        for i in range(quarters):
            if p < PARTS:
                gathered.append(jnp.concatenate([recv_b[p, 4 * i + k] for k in range(4)], axis=1))
            else:
                rest = jnp.concatenate([recv_c[4 * i + k] for k in range(4)], axis=1)
                gathered.append(jnp.concatenate([rest, pad], axis=0).astype(BF16))
        gathered = jnp.concatenate(gathered, axis=0)
        natural = nn(gathered, pi_tab[...])
        for i in range(2 * p, min(2 * p + 2, (cap + 1) // 2)):
            r0 = 8 * (i - 2 * p)
            north, south = [], []
            for b in range(blocks):
                xx, gg = b // quarters, b % quarters
                north.append(natural[gg * ROWS + r0 : gg * ROWS + r0 + 8, xx * 128 : xx * 128 + 128])
                xx, gg = NX - 1 - xx, quarters - 1 - gg
                south.append(natural[gg * ROWS + r0 : gg * ROWS + r0 + 8, xx * 128 : xx * 128 + 128])
            both = jnp.concatenate(
                [jnp.concatenate(north, axis=1), jnp.concatenate(south, axis=1)], axis=0
            ).astype(BF16)
            raws = []
            for k in (2 * i, 2 * i + 1):
                if k < cap:
                    out = nt(both, basis[k])
                    raws.append(out[:8] + parity * out[8:])
            raw = jnp.where(first, raws[0], raws[1] if len(raws) > 1 else 0.0)
            spectral = raw * damp[pl.ds(8 * i, 8), :]
            for k in (2 * i, 2 * i + 1):
                if k < cap:
                    at = 4 * (k - 2 * i)
                    for f in range(2):
                        spec_ref[k, 0, f] = spectral[at + 2 * f : at + 2 * f + 2]
            rounded = spectral.astype(BF16).astype(F32)
            pair = jnp.concatenate([rounded, rounded * parity], axis=0).astype(BF16)
            outs = [nn(pair, basis[k]) for k in (2 * i, 2 * i + 1) if k < cap]
            keep = jnp.concatenate([first, first], axis=0)
            synth = jnp.where(keep, outs[0], outs[1] if len(outs) > 1 else 0.0)
            synth = synth * (1.0 / math.sqrt(degrees))
            for b in range(blocks):
                xx, gg = b // quarters, b % quarters
                back_t[p, pl.ds(gg * ROWS + r0, 8), pl.ds(xx * 128, 128)] = synth[:8, b * 128 : b * 128 + 128]
                xx, gg = NX - 1 - xx, quarters - 1 - gg
                back_t[p, pl.ds(gg * ROWS + r0, 8), pl.ds(xx * 128, 128)] = synth[8:, b * 128 : b * 128 + 128]
        for gg in range(quarters):
            if 2 * p + 2 > (cap + 1) // 2:
                back_t[p, pl.ds(gg * ROWS + 8, 8), :] = jnp.zeros((8, 512), F32)
        mixed = nt(back_t[p].astype(BF16), pi_tab[...])
        for zz in range(NZ):
            piece = mixed[zz // 4 * ROWS : zz // 4 * ROWS + ROWS, zz % 4 * 128 : zz % 4 * 128 + 128]
            if p < PARTS:
                send_b2[p, zz] = piece.astype(BF16)
            else:
                send_c2[zz] = piece[:REST]
        back[p][0]()
        if p < PARTS:
            recv_b2[p, z] = send_b2[p, z]
        else:
            recv_c2[z] = send_c2[z]

    joined = 0.0
    for p in range(PARTS):
        back[p][1]()
        rows = NZ * ROWS
        joined += tn(recv_b2[p].reshape(rows, 128), e_tab[pl.ds(p * rows, rows), :])
    back[PARTS][1]()
    rest = jnp.concatenate([recv_c2[zz] for zz in range(NZ)], axis=0).astype(BF16)
    joined += tn(rest, e_tab[pl.ds(full, NZ * REST), :])
    send_a2[...] = joined.astype(BF16).reshape(GROUPS, 16, 512)
    start, wait, left5 = exchange(send_a2, recv_a2, sa2, ra2, in_group, group, GROUPS)
    start()
    recv_a2[group] = send_a2[group]
    wait()

    by_part = jnp.concatenate(
        [
            jnp.concatenate([recv_a2[g, :, pl.ds(b * 128, 128)] for g in range(GROUPS)], axis=1)
            for b in range(4)
        ],
        axis=0,
    )
    waved = nn(by_part, onehot[...])
    weight = jnp.where(lax.broadcasted_iota(jnp.int32, (1, 1024), 1) == 0, 1.0, 2.0)
    waved = (waved * weight).astype(BF16)
    parts = []
    for j in range(4):
        lhs = jnp.concatenate(
            [waved[:32, j * 256 : j * 256 + 256], waved[32:, j * 256 : j * 256 + 256]], axis=1
        )
        out = nt(lhs, hi[j]) + nt(lhs, lo[j])
        parts.append((out[:, :sector], out[:, sector:]))
    (u0, u4), (u1, v1), (u2, v2), (u3, v3) = parts
    even, odd = u0 + u4, u0 - u4
    ud, us = HALF * (u1 - u3), u1 + u3
    vd, vs = v1 - v3, HALF * (v1 + v3)
    grid = (
        even + us + u2,
        odd + ud - vs - v2,
        even - u2 - vd,
        odd - ud - vs + v2,
        even - us + u2,
        odd - ud + vs - v2,
        even - u2 + vd,
        odd + ud + vs + v2,
    )
    for s in range(SECTORS):
        send_l2[s] = jnp.concatenate([grid[s][:16], grid[s][16:]], axis=1).astype(BF16)
    start, wait, left6 = exchange(send_l2, recv_l2, sl2, rl2, in_sector, lon, SECTORS)
    start()
    recv_l2[lon] = send_l2[lon]
    wait()
    for s in range(SECTORS):
        both = recv_l2[s].astype(F32)
        tend_ref[s, 0] = both[:, :sector]
        tend_ref[s, 1] = both[:, sector:]
    for left in (left1, left2, left5, left6, *(e[2] for e in there), *(e[2] for e in back)):
        left()


def body(wind_u, wind_v, basis, wave_slots, degree_count, viscosity):
    levels, lat_rows, sector = wind_u.shape
    cap, degrees, half_lat = basis.shape
    waves = wave_slots.shape[0]
    high, low = dft_table(sector * SECTORS, waves)
    vmem = pl.BlockSpec(memory_space=pltpu.VMEM)
    hbm = pl.BlockSpec(memory_space=pltpu.HBM)
    dma = pltpu.SemaphoreType.DMA
    return pl.pallas_call(
        kernel,
        out_shape=(
            jax.ShapeDtypeStruct((cap, 1, 2, 2, degrees), F32),
            jax.ShapeDtypeStruct((levels, 2, lat_rows, sector), F32),
        ),
        in_specs=[hbm] * 11,
        out_specs=(vmem, vmem),
        scratch_shapes=[
            pltpu.VMEM(wind_u.shape, F32),
            pltpu.VMEM(wind_v.shape, F32),
            pltpu.VMEM((waves,), jnp.int32),
            pltpu.VMEM((waves,), jnp.int32),
            pltpu.VMEM((levels,), F32),
            pltpu.VMEM((waves, 1024), BF16),
            pltpu.VMEM(basis.shape, BF16),
            pltpu.VMEM(high.shape, BF16),
            pltpu.VMEM(low.shape, BF16),
            pltpu.VMEM((PARTS * NZ * ROWS + NZ * REST, 512), BF16),
            pltpu.VMEM((512, 512), BF16),
            pltpu.VMEM((1024, 1024), BF16),
            pltpu.VMEM((40, degrees), F32),
            pltpu.VMEM((SECTORS, lat_rows, 2 * sector), F32),
            pltpu.VMEM((SECTORS, lat_rows, 2 * sector), F32),
            pltpu.VMEM((GROUPS, 16, 512), BF16),
            pltpu.VMEM((GROUPS, 16, 512), BF16),
            pltpu.VMEM((PARTS, NZ, ROWS, 128), BF16),
            pltpu.VMEM((PARTS, NZ, ROWS, 128), BF16),
            pltpu.VMEM((64, 1024), BF16),
            pltpu.VMEM((PARTS + 1, NZ // 4 * ROWS, 512), F32),
            pltpu.VMEM((PARTS, NZ, ROWS, 128), BF16),
            pltpu.VMEM((PARTS, NZ, ROWS, 128), BF16),
            pltpu.VMEM((NZ, REST, 128), F32),
            pltpu.VMEM((NZ, REST, 128), F32),
            pltpu.VMEM((NZ, REST, 128), F32),
            pltpu.VMEM((NZ, REST, 128), F32),
            pltpu.VMEM((GROUPS, 16, 512), BF16),
            pltpu.VMEM((GROUPS, 16, 512), BF16),
            pltpu.VMEM((SECTORS, lat_rows, 2 * sector), BF16),
            pltpu.VMEM((SECTORS, lat_rows, 2 * sector), BF16),
            dma((11,)),
        ]
        + [dma(())] * 4 + [dma((PARTS + 1,))] * 4 + [dma(())] * 4,
        compiler_params=pltpu.CompilerParams(
            collective_id=0, has_side_effects=True, vmem_limit_bytes=40 * 2**20
        ),
    )(
        *(
            pltpu.with_memory_space_constraint(operand, pltpu.HBM)
            for operand in (
                wind_u,
                wind_v,
                wave_slots,
                degree_count,
                viscosity,
                basis,
                jnp.asarray(high),
                jnp.asarray(low),
                jnp.asarray(spread_table(cap)),
                jnp.asarray(lane_table()),
                jnp.asarray(order_table(waves)),
            )
        )
    )


def solution(mesh):
    return jax.shard_map(
        body,
        mesh=mesh,
        in_specs=(
            P(None, "lat", "lon"),
            P(None, "lat", "lon"),
            P("lat", None, None),
            P(),
            P(),
            P(),
        ),
        out_specs=(P("lat", "lon", None, None, None), P(None, None, "lat", "lon")),
        check_vma=False,
    )
```

```python
import functools
import math

import jax
import jax.numpy as jnp
import ml_dtypes
import numpy as np
from jax import lax
from jax.experimental import pallas as pl
from jax.experimental.pallas import tpu as pltpu
from jax.sharding import PartitionSpec as P

MESH = pl.DeviceIdType.MESH
F32 = jnp.float32
BF16 = jnp.bfloat16

NX, NZ, NC = 4, 12, 2
GROUPS = NX * NC
SECTORS = 8
PARTS = 2
ROWS = 16
REST = 4
HALF = math.sqrt(0.5)


def nt(a, b):
    return lax.dot_general(a, b, (((1,), (1,)), ((), ())), preferred_element_type=F32)


def nn(a, b):
    return lax.dot_general(a, b, (((1,), (0,)), ((), ())), preferred_element_type=F32)


def tn(a, b):
    return lax.dot_general(a, b, (((0,), (0,)), ((), ())), preferred_element_type=F32)


@functools.cache
def wave_lanes(waves):
    per = waves // SECTORS
    out = np.full((4, 256), -1, np.int64)
    for j in range(4):
        other = 4 if j == 0 else SECTORS - j
        out[j, :per] = SECTORS * np.arange(per) + j
        out[j, per : 2 * per] = SECTORS * np.arange(per) + other
    return out


@functools.cache
def dft_table(length, waves):
    sector = length // SECTORS
    per = waves // SECTORS
    lanes = wave_lanes(waves)
    t = np.arange(sector)
    table = np.zeros((4, 2, sector, 2, 256), np.float64)
    for j in range(4):
        m = lanes[j, : 2 * per]
        angle = 2.0 * math.pi * ((t[:, None] * m[None, :]) % length) / length
        c, s = np.cos(angle), np.sin(angle)
        if j == 0:
            table[j, 0, :, 0, :per] = c[:, :per]
            table[j, 0, :, 1, :per] = -s[:, :per]
            table[j, 1, :, 0, per : 2 * per] = c[:, per:]
            table[j, 1, :, 1, per : 2 * per] = -s[:, per:]
        else:
            sign = np.where(np.arange(2 * per) < per, 1.0, -1.0)
            table[j, 0, :, 0, : 2 * per] = c
            table[j, 0, :, 1, : 2 * per] = -s
            table[j, 1, :, 0, : 2 * per] = s * sign
            table[j, 1, :, 1, : 2 * per] = c * sign
    table = table.reshape(4, 2 * sector, 512) / math.sqrt(length)
    high = table.astype(ml_dtypes.bfloat16)
    low = (table - high.astype(np.float64)).astype(ml_dtypes.bfloat16)
    return high, low


@functools.cache
def order_table(waves):
    lanes = wave_lanes(waves).reshape(1024)
    return (np.arange(waves)[:, None] == lanes[None, :]).astype(ml_dtypes.bfloat16)


@functools.cache
def spread_table(cap):
    e = np.zeros((PARTS, NZ, ROWS, 4, 128), np.float32)
    rest = np.zeros((NZ, REST, 4, 128), np.float32)
    for z in range(NZ):
        for k in range(cap):
            for f in range(2):
                for r in range(2):
                    rows = e[k // 4] if k < 4 * PARTS else rest
                    rows[z, k % 4 * 4 + f * 2 + r, r * 2 + f, z * cap + k] = 1.0
    both = np.concatenate([e.reshape(PARTS * NZ * ROWS, 512), rest.reshape(NZ * REST, 512)])
    return both.astype(ml_dtypes.bfloat16)


@functools.cache
def lane_table():
    p = np.zeros((512, 512), np.float32)
    for z in range(4):
        for x in range(NX):
            for c in range(NC):
                for i in range(16):
                    lane = z * 32 + c * 16 + i
                    if x >= NX // 2:
                        lane = 127 - lane
                    p[z * 128 + (x * NC + c) * 16 + i, x * 128 + lane] = 1.0
    return p.astype(ml_dtypes.bfloat16)


def kernel(
    u_hbm, v_hbm, ws_hbm, cnt_hbm, visc_hbm, basis_hbm, hi_hbm, lo_hbm, e_hbm, pi_hbm, order_hbm, hi_t_hbm, pi_t_hbm,
    spec_ref, tend_ref,
    u_ref, v_ref, ws_ref, cnt_ref, visc_ref, order, basis, hi, lo, e_tab, pi_tab, hi_t, pi_t, onehot, damp,
    send_l, recv_l, send_a, recv_a, send_b, recv_b, turned,
    back_t, send_b2, recv_b2, send_c, recv_c, send_c2, recv_c2, send_a2, recv_a2, send_l2, recv_l2,
    load_sem, sl, rl, sa, ra, sb, rb, sb2, rb2, sa2, ra2, sl2, rl2,
):
    lat = lax.axis_index("lat")
    lon = lax.axis_index("lon")
    x = lat // (NZ * NC)
    z = lat // NC % NZ
    core = lat % NC
    group = x * NC + core
    cap, degrees, half_lat = basis.shape
    waves = ws_ref.shape[0]
    sector = u_ref.shape[2]

    def in_group(g):
        return (g // NC * (NZ * NC) + z * NC + g % NC, lon)

    def in_column(zz):
        return (lat + (zz - z) * NC, lon)

    def in_sector(s):
        return (lat, s)

    def partners(me, n):
        for d in sorted(range(1, n), key=lambda d: -min(d, n - d)):
            to = me + d
            yield jnp.where(to >= n, to - n, to)

    loads = [
        pltpu.make_async_copy(src, dst, load_sem.at[i])
        for i, (src, dst) in enumerate(
            (
                (u_hbm, u_ref), (v_hbm, v_ref), (ws_hbm, ws_ref), (cnt_hbm, cnt_ref), (visc_hbm, visc_ref),
                (order_hbm, order), (hi_hbm, hi), (lo_hbm, lo), (e_hbm, e_tab), (pi_hbm, pi_tab), (basis_hbm, basis),
                (pi_t_hbm, pi_t), (hi_t_hbm, hi_t),
            )
        )
    ]
    for load in loads[:2]:
        load.start()

    barrier = pltpu.get_barrier_semaphore()

    def greet(device_of, me, n):
        for to in partners(me, n):
            pl.semaphore_signal(barrier, inc=1, device_id=device_of(to), device_id_type=MESH)

    greet(in_sector, lon, SECTORS)
    greet(in_group, group, GROUPS)
    greet(in_column, z, NZ)

    for load in loads[2:]:
        load.start()
    loads[0].wait()
    loads[1].wait()

    pl.semaphore_wait(barrier, SECTORS + GROUPS + NZ - 3)

    def exchange(src, dst, send_sem, recv_sem, device_of, me, n):
        def start(prepare=None):
            for to in partners(me, n):
                if prepare is not None:
                    prepare(to)
                pltpu.make_async_remote_copy(
                    src_ref=src.at[to],
                    dst_ref=dst.at[me],
                    send_sem=send_sem,
                    recv_sem=recv_sem,
                    device_id=device_of(to),
                    device_id_type=MESH,
                ).start()

        def landed():
            whole = dst.at[pl.ds(0, n - 1)]
            pltpu.make_async_copy(whole, whole, recv_sem).wait()

        def left():
            whole = src.at[pl.ds(0, n - 1)]
            pltpu.make_async_copy(whole, whole, send_sem).wait()

        return start, landed, left

    def products(level):
        u = u_ref[level]
        v = v_ref[level]
        return jnp.concatenate([u * v, u * u - v * v], axis=1)

    def prepare(level):
        send_l[level] = products(level)

    start, wait, left1 = exchange(send_l, recv_l, sl, rl, in_sector, lon, SECTORS)
    start(prepare)
    recv_l[lon] = products(lon)

    for load in loads[2:6]:
        load.wait()
    ws = ws_ref[...].reshape(1, waves)
    owner = ws // cap
    lane = (owner // (NZ * NC) * NC + owner % NC) * 128 + owner // NC % NZ * cap + ws % cap
    digit = lax.broadcasted_iota(jnp.int32, (16, waves), 0)
    digits = jnp.where(digit == 0, lane // 32, jnp.where(digit == 1, lane % 32, 1)).astype(F32)
    ordered = nn(digits.astype(BF16), order[...])
    target = (ordered[0:1] * 32.0 + ordered[1:2] + ordered[2:3] - 1.0).astype(jnp.int32)
    for b in range(GROUPS):
        ids = lax.broadcasted_iota(jnp.int32, (128, 1024), 0) + b * 128
        onehot[pl.ds(b * 128, 128), :] = jnp.where(ids == target, 1.0, 0.0).astype(BF16)

    rows40 = damp.shape[0]
    slot = lax.broadcasted_iota(jnp.int32, (rows40, waves), 0) // 4
    here = (ws == lat * cap + slot) & (slot < cap)
    wave_ids = lax.broadcasted_iota(jnp.int32, (rows40, waves), 1)
    wave_here = jnp.sum(jnp.where(here, wave_ids, 0).astype(F32), axis=1, keepdims=True)
    kept_here = jnp.sum(jnp.where(here, cnt_ref[...].reshape(1, waves), 0).astype(F32), axis=1, keepdims=True)
    levels = lax.broadcasted_iota(jnp.int32, (1, SECTORS), 1)
    rate = jnp.sum(jnp.where(levels == lon, visc_ref[...].reshape(1, SECTORS), 0.0), axis=1, keepdims=True)
    degree = lax.broadcasted_iota(jnp.int32, (rows40, degrees), 1).astype(F32)
    total = wave_here + degree
    q = total * (total + 1.0) / float(degrees * (degrees + 1))
    damping = (1.0 / math.sqrt(2 * half_lat)) / (1.0 + rate * (q * q))
    damp[...] = jnp.where(degree < kept_here, damping, 0.0)

    wait()
    loads[6].wait()
    loads[7].wait()

    a = [recv_l[s] for s in range(SECTORS)]
    e0, e1, e2, e3 = (a[i] + a[i + 4] for i in range(4))
    o0, o1, o2, o3 = (a[i] - a[i + 4] for i in range(4))
    od = HALF * (o1 - o3)
    os = HALF * (o1 + o3)
    sums = (
        (e0 + e1 + e2 + e3, e0 - e1 + e2 - e3),
        (o0 + od, -(os + o2)),
        (e0 - e2, e3 - e1),
        (o0 - od, o2 - os),
    )
    for j in range(4):
        one, two = sums[j]
        both = jnp.concatenate(
            [
                jnp.concatenate([one[:, :sector], two[:, :sector]], axis=1),
                jnp.concatenate([one[:, sector:], two[:, sector:]], axis=1),
            ],
            axis=0,
        )
        high = both.astype(BF16)
        low = (both - high.astype(F32)).astype(BF16)
        two = nn(jnp.concatenate([high, low], axis=0), hi[j])
        four = two[:32] + two[32:] + nn(high, lo[j])
        turned[0:32, pl.ds(j * 256, 256)] = four[:, :256].astype(BF16)
        turned[32:64, pl.ds(j * 256, 256)] = four[:, 256:].astype(BF16)

    placed = nt(turned[...], onehot[...]).astype(BF16)
    for g in range(GROUPS):
        for b in range(4):
            send_a[g, :, pl.ds(b * 128, 128)] = placed[b * 16 : b * 16 + 16, g * 128 : g * 128 + 128]
    start, wait, left2 = exchange(send_a, recv_a, sa, ra, in_group, group, GROUPS)
    start()
    recv_a[group] = send_a[group]
    loads[8].wait()
    wait()
    spread = nt(e_tab[...], recv_a[...].reshape(GROUPS * 16, 512))
    full = PARTS * NZ * ROWS
    send_b[...] = spread[:full].astype(BF16).reshape(PARTS, NZ, ROWS, 128)
    for zz in range(NZ):
        send_c[zz] = spread[full + REST * zz : full + REST * zz + REST]

    def over_z(src, dst, send_sems, recv_sems, rest_src, rest_dst):
        pieces = [(src.at[p], dst.at[p]) for p in range(PARTS)] + [(rest_src, rest_dst)]
        return [
            exchange(a, b, send_sems.at[p], recv_sems.at[p], in_column, z, NZ)
            for p, (a, b) in enumerate(pieces)
        ]

    there = over_z(send_b, recv_b, sb, rb, send_c, recv_c)
    back = over_z(send_b2, recv_b2, sb2, rb2, send_c2, recv_c2)
    for p in range(PARTS + 1):
        there[p][0]()
    for p in range(PARTS):
        recv_b[p, z] = send_b[p, z]
    recv_c[z] = send_c[z]
    for load in loads[9:]:
        load.wait()

    quarters = NZ // 4
    parity = jnp.where(lax.broadcasted_iota(jnp.int32, (8, degrees), 1) % 2 == 0, 1.0, -1.0)
    first = lax.broadcasted_iota(jnp.int32, (8, 1), 0) < 4
    blocks = half_lat // 128
    pad = jnp.zeros((ROWS - REST, 512), F32)
    for p in range(PARTS + 1):
        there[p][1]()
        gathered = []
        for i in range(quarters):
            if p < PARTS:
                gathered.append(jnp.concatenate([recv_b[p, 4 * i + k] for k in range(4)], axis=1))
            else:
                rest = jnp.concatenate([recv_c[4 * i + k] for k in range(4)], axis=1)
                gathered.append(jnp.concatenate([rest, pad], axis=0).astype(BF16))
        gathered = jnp.concatenate(gathered, axis=0)
        natural = nn(gathered, pi_tab[...])
        for i in range(2 * p, min(2 * p + 2, (cap + 1) // 2)):
            r0 = 8 * (i - 2 * p)
            north, south = [], []
            for b in range(blocks):
                xx, gg = b // quarters, b % quarters
                north.append(natural[gg * ROWS + r0 : gg * ROWS + r0 + 8, xx * 128 : xx * 128 + 128])
                xx, gg = NX - 1 - xx, quarters - 1 - gg
                south.append(natural[gg * ROWS + r0 : gg * ROWS + r0 + 8, xx * 128 : xx * 128 + 128])
            both = jnp.concatenate(
                [jnp.concatenate(north, axis=1), jnp.concatenate(south, axis=1)], axis=0
            ).astype(BF16)
            raws = []
            for k in (2 * i, 2 * i + 1):
                if k < cap:
                    out = nt(both, basis[k])
                    raws.append(out[:8] + parity * out[8:])
            raw = jnp.where(first, raws[0], raws[1] if len(raws) > 1 else 0.0)
            spectral = raw * damp[pl.ds(8 * i, 8), :]
            for k in (2 * i, 2 * i + 1):
                if k < cap:
                    at = 4 * (k - 2 * i)
                    for f in range(2):
                        spec_ref[k, 0, f] = spectral[at + 2 * f : at + 2 * f + 2]
            rounded = spectral.astype(BF16).astype(F32)
            pair = jnp.concatenate([rounded, rounded * parity], axis=0).astype(BF16)
            outs = [nn(pair, basis[k]) for k in (2 * i, 2 * i + 1) if k < cap]
            keep = jnp.concatenate([first, first], axis=0)
            synth = jnp.where(keep, outs[0], outs[1] if len(outs) > 1 else 0.0)
            synth = synth * (1.0 / math.sqrt(degrees))
            for b in range(blocks):
                xx, gg = b // quarters, b % quarters
                back_t[p, pl.ds(gg * ROWS + r0, 8), pl.ds(xx * 128, 128)] = synth[:8, b * 128 : b * 128 + 128]
                xx, gg = NX - 1 - xx, quarters - 1 - gg
                back_t[p, pl.ds(gg * ROWS + r0, 8), pl.ds(xx * 128, 128)] = synth[8:, b * 128 : b * 128 + 128]
        for gg in range(quarters):
            if 2 * p + 2 > (cap + 1) // 2:
                back_t[p, pl.ds(gg * ROWS + 8, 8), :] = jnp.zeros((8, 512), F32)
        mixed = nn(back_t[p].astype(BF16), pi_t[...])
        for zz in range(NZ):
            piece = mixed[zz // 4 * ROWS : zz // 4 * ROWS + ROWS, zz % 4 * 128 : zz % 4 * 128 + 128]
            if p < PARTS:
                send_b2[p, zz] = piece.astype(BF16)
            else:
                send_c2[zz] = piece[:REST]
        back[p][0]()
        if p < PARTS:
            recv_b2[p, z] = send_b2[p, z]
        else:
            recv_c2[z] = send_c2[z]

    joined = 0.0
    for p in range(PARTS):
        back[p][1]()
        rows = NZ * ROWS
        joined += tn(recv_b2[p].reshape(rows, 128), e_tab[pl.ds(p * rows, rows), :])
    back[PARTS][1]()
    rest = jnp.concatenate([recv_c2[zz] for zz in range(NZ)], axis=0).astype(BF16)
    joined += tn(rest, e_tab[pl.ds(full, NZ * REST), :])
    send_a2[...] = joined.astype(BF16).reshape(GROUPS, 16, 512)
    start, wait, left5 = exchange(send_a2, recv_a2, sa2, ra2, in_group, group, GROUPS)
    start()
    recv_a2[group] = send_a2[group]
    wait()

    by_part = jnp.concatenate(
        [
            jnp.concatenate([recv_a2[g, :, pl.ds(b * 128, 128)] for g in range(GROUPS)], axis=1)
            for b in range(4)
        ],
        axis=0,
    )
    waved = nn(by_part, onehot[...])
    weight = jnp.where(lax.broadcasted_iota(jnp.int32, (1, 1024), 1) == 0, 1.0, 2.0)
    waved = (waved * weight).astype(BF16)
    parts = []
    for j in range(4):
        lhs = jnp.concatenate(
            [waved[:32, j * 256 : j * 256 + 256], waved[32:, j * 256 : j * 256 + 256]], axis=1
        )
        out = nn(lhs, hi_t[j])
        parts.append((out[:, :sector], out[:, sector:]))
    (u0, u4), (u1, v1), (u2, v2), (u3, v3) = parts
    even, odd = u0 + u4, u0 - u4
    ud, us = HALF * (u1 - u3), u1 + u3
    vd, vs = v1 - v3, HALF * (v1 + v3)
    grid = (
        even + us + u2,
        odd + ud - vs - v2,
        even - u2 - vd,
        odd - ud - vs + v2,
        even - us + u2,
        odd - ud + vs - v2,
        even - u2 + vd,
        odd + ud + vs + v2,
    )
    for s in range(SECTORS):
        send_l2[s] = jnp.concatenate([grid[s][:16], grid[s][16:]], axis=1).astype(BF16)
    start, wait, left6 = exchange(send_l2, recv_l2, sl2, rl2, in_sector, lon, SECTORS)
    start()
    recv_l2[lon] = send_l2[lon]
    wait()
    for s in range(SECTORS):
        both = recv_l2[s].astype(F32)
        tend_ref[s, 0] = both[:, :sector]
        tend_ref[s, 1] = both[:, sector:]
    for left in (left1, left2, left5, left6, *(e[2] for e in there), *(e[2] for e in back)):
        left()


def body(wind_u, wind_v, basis, wave_slots, degree_count, viscosity):
    levels, lat_rows, sector = wind_u.shape
    cap, degrees, half_lat = basis.shape
    waves = wave_slots.shape[0]
    high, low = dft_table(sector * SECTORS, waves)
    vmem = pl.BlockSpec(memory_space=pltpu.VMEM)
    hbm = pl.BlockSpec(memory_space=pltpu.HBM)
    dma = pltpu.SemaphoreType.DMA
    return pl.pallas_call(
        kernel,
        out_shape=(
            jax.ShapeDtypeStruct((cap, 1, 2, 2, degrees), F32),
            jax.ShapeDtypeStruct((levels, 2, lat_rows, sector), F32),
        ),
        in_specs=[hbm] * 13,
        out_specs=(vmem, vmem),
        scratch_shapes=[
            pltpu.VMEM(wind_u.shape, F32),
            pltpu.VMEM(wind_v.shape, F32),
            pltpu.VMEM((waves,), jnp.int32),
            pltpu.VMEM((waves,), jnp.int32),
            pltpu.VMEM((levels,), F32),
            pltpu.VMEM((waves, 1024), BF16),
            pltpu.VMEM(basis.shape, BF16),
            pltpu.VMEM(high.shape, BF16),
            pltpu.VMEM(low.shape, BF16),
            pltpu.VMEM((PARTS * NZ * ROWS + NZ * REST, 512), BF16),
            pltpu.VMEM((512, 512), BF16),
            pltpu.VMEM((high.shape[0], high.shape[2], high.shape[1]), BF16),
            pltpu.VMEM((512, 512), BF16),
            pltpu.VMEM((1024, 1024), BF16),
            pltpu.VMEM((40, degrees), F32),
            pltpu.VMEM((SECTORS, lat_rows, 2 * sector), F32),
            pltpu.VMEM((SECTORS, lat_rows, 2 * sector), F32),
            pltpu.VMEM((GROUPS, 16, 512), BF16),
            pltpu.VMEM((GROUPS, 16, 512), BF16),
            pltpu.VMEM((PARTS, NZ, ROWS, 128), BF16),
            pltpu.VMEM((PARTS, NZ, ROWS, 128), BF16),
            pltpu.VMEM((64, 1024), BF16),
            pltpu.VMEM((PARTS + 1, NZ // 4 * ROWS, 512), F32),
            pltpu.VMEM((PARTS, NZ, ROWS, 128), BF16),
            pltpu.VMEM((PARTS, NZ, ROWS, 128), BF16),
            pltpu.VMEM((NZ, REST, 128), F32),
            pltpu.VMEM((NZ, REST, 128), F32),
            pltpu.VMEM((NZ, REST, 128), F32),
            pltpu.VMEM((NZ, REST, 128), F32),
            pltpu.VMEM((GROUPS, 16, 512), BF16),
            pltpu.VMEM((GROUPS, 16, 512), BF16),
            pltpu.VMEM((SECTORS, lat_rows, 2 * sector), BF16),
            pltpu.VMEM((SECTORS, lat_rows, 2 * sector), BF16),
            dma((13,)),
        ]
        + [dma(())] * 4 + [dma((PARTS + 1,))] * 4 + [dma(())] * 4,
        compiler_params=pltpu.CompilerParams(
            collective_id=0, has_side_effects=True, vmem_limit_bytes=40 * 2**20
        ),
    )(
        *(
            pltpu.with_memory_space_constraint(operand, pltpu.HBM)
            for operand in (
                wind_u,
                wind_v,
                wave_slots,
                degree_count,
                viscosity,
                basis,
                jnp.asarray(high),
                jnp.asarray(low),
                jnp.asarray(spread_table(cap)),
                jnp.asarray(lane_table()),
                jnp.asarray(order_table(waves)),
                jnp.asarray(np.ascontiguousarray(high.transpose(0, 2, 1))),
                jnp.asarray(np.ascontiguousarray(lane_table().T)),
            )
        )
    )


def solution(mesh):
    return jax.shard_map(
        body,
        mesh=mesh,
        in_specs=(
            P(None, "lat", "lon"),
            P(None, "lat", "lon"),
            P("lat", None, None),
            P(),
            P(),
            P(),
        ),
        out_specs=(P("lat", "lon", None, None, None), P(None, None, "lat", "lon")),
        check_vma=False,
    )
```

```python
import functools
import math

import jax
import jax.numpy as jnp
import ml_dtypes
import numpy as np
from jax import lax
from jax.experimental import pallas as pl
from jax.experimental.pallas import tpu as pltpu
from jax.sharding import PartitionSpec as P

MESH = pl.DeviceIdType.MESH
F32 = jnp.float32
BF16 = jnp.bfloat16

NX, NZ, NC = 4, 12, 2
GROUPS = NX * NC
SECTORS = 8
PARTS = 2
ROWS = 16
REST = 4
HALF = math.sqrt(0.5)


def nt(a, b):
    return lax.dot_general(a, b, (((1,), (1,)), ((), ())), preferred_element_type=F32)


def nn(a, b):
    return lax.dot_general(a, b, (((1,), (0,)), ((), ())), preferred_element_type=F32)


def tn(a, b):
    return lax.dot_general(a, b, (((0,), (0,)), ((), ())), preferred_element_type=F32)


@functools.cache
def wave_lanes(waves):
    per = waves // SECTORS
    out = np.full((4, 256), -1, np.int64)
    for j in range(4):
        other = 4 if j == 0 else SECTORS - j
        out[j, :per] = SECTORS * np.arange(per) + j
        out[j, per : 2 * per] = SECTORS * np.arange(per) + other
    return out


@functools.cache
def dft_table(length, waves):
    sector = length // SECTORS
    per = waves // SECTORS
    lanes = wave_lanes(waves)
    t = np.arange(sector)
    table = np.zeros((4, 2, sector, 2, 256), np.float64)
    for j in range(4):
        m = lanes[j, : 2 * per]
        angle = 2.0 * math.pi * ((t[:, None] * m[None, :]) % length) / length
        c, s = np.cos(angle), np.sin(angle)
        if j == 0:
            table[j, 0, :, 0, :per] = c[:, :per]
            table[j, 0, :, 1, :per] = -s[:, :per]
            table[j, 1, :, 0, per : 2 * per] = c[:, per:]
            table[j, 1, :, 1, per : 2 * per] = -s[:, per:]
        else:
            sign = np.where(np.arange(2 * per) < per, 1.0, -1.0)
            table[j, 0, :, 0, : 2 * per] = c
            table[j, 0, :, 1, : 2 * per] = -s
            table[j, 1, :, 0, : 2 * per] = s * sign
            table[j, 1, :, 1, : 2 * per] = c * sign
    table = table.reshape(4, 2 * sector, 512) / math.sqrt(length)
    high = table.astype(ml_dtypes.bfloat16)
    low = (table - high.astype(np.float64)).astype(ml_dtypes.bfloat16)
    return high, low


@functools.cache
def order_table(waves):
    lanes = wave_lanes(waves).reshape(1024)
    return (np.arange(waves)[:, None] == lanes[None, :]).astype(ml_dtypes.bfloat16)


@functools.cache
def spread_table(cap):
    e = np.zeros((PARTS, NZ, ROWS, 4, 128), np.float32)
    rest = np.zeros((NZ, REST, 4, 128), np.float32)
    for z in range(NZ):
        for k in range(cap):
            for f in range(2):
                for r in range(2):
                    rows = e[k // 4] if k < 4 * PARTS else rest
                    rows[z, k % 4 * 4 + f * 2 + r, r * 2 + f, z * cap + k] = 1.0
    both = np.concatenate([e.reshape(PARTS * NZ * ROWS, 512), rest.reshape(NZ * REST, 512)])
    return both.astype(ml_dtypes.bfloat16)


@functools.cache
def lane_table():
    p = np.zeros((512, 512), np.float32)
    for z in range(4):
        for x in range(NX):
            for c in range(NC):
                for i in range(16):
                    lane = z * 32 + c * 16 + i
                    if x >= NX // 2:
                        lane = 127 - lane
                    p[z * 128 + (x * NC + c) * 16 + i, x * 128 + lane] = 1.0
    return p.astype(ml_dtypes.bfloat16)


def kernel(
    u_hbm, v_hbm, ws_hbm, cnt_hbm, visc_hbm, basis_hbm, hi_hbm, lo_hbm, e_hbm, pi_hbm, order_hbm, hi_t_hbm, pi_t_hbm,
    spec_ref, tend_ref,
    u_ref, v_ref, ws_ref, cnt_ref, visc_ref, order, basis, hi, lo, e_tab, pi_tab, hi_t, pi_t, onehot, damp,
    send_l, recv_l, send_a, recv_a, send_b, recv_b, turned,
    back_t, send_b2, recv_b2, send_c, recv_c, send_c2, recv_c2, send_a2, recv_a2, send_l2, recv_l2,
    load_sem, sl, rl, sa, ra, sb, rb, sb2, rb2, sa2, ra2, sl2, rl2,
):
    lat = lax.axis_index("lat")
    lon = lax.axis_index("lon")
    x = lat // (NZ * NC)
    z = lat // NC % NZ
    core = lat % NC
    group = x * NC + core
    cap, degrees, half_lat = basis.shape
    waves = ws_ref.shape[0]
    sector = u_ref.shape[2]

    def in_group(g):
        return (g // NC * (NZ * NC) + z * NC + g % NC, lon)

    def in_column(zz):
        return (lat + (zz - z) * NC, lon)

    def in_sector(s):
        return (lat, s)

    def partners(me, n):
        for d in sorted(range(1, n), key=lambda d: -min(d, n - d)):
            to = me + d
            yield jnp.where(to >= n, to - n, to)

    loads = [
        pltpu.make_async_copy(src, dst, load_sem.at[i])
        for i, (src, dst) in enumerate(
            (
                (u_hbm, u_ref), (v_hbm, v_ref), (ws_hbm, ws_ref), (cnt_hbm, cnt_ref), (visc_hbm, visc_ref),
                (order_hbm, order), (hi_hbm, hi), (lo_hbm, lo), (e_hbm, e_tab), (pi_hbm, pi_tab), (basis_hbm, basis),
                (pi_t_hbm, pi_t), (hi_t_hbm, hi_t),
            )
        )
    ]
    for load in loads[:2]:
        load.start()

    barrier = pltpu.get_barrier_semaphore()

    def greet(device_of, me, n):
        for to in partners(me, n):
            pl.semaphore_signal(barrier, inc=1, device_id=device_of(to), device_id_type=MESH)

    greet(in_sector, lon, SECTORS)
    greet(in_group, group, GROUPS)
    greet(in_column, z, NZ)

    for load in loads[2:]:
        load.start()
    loads[0].wait()
    loads[1].wait()

    pl.semaphore_wait(barrier, SECTORS + GROUPS + NZ - 3)

    def exchange(src, dst, send_sem, recv_sem, device_of, me, n):
        def start(prepare=None):
            for to in partners(me, n):
                if prepare is not None:
                    prepare(to)
                pltpu.make_async_remote_copy(
                    src_ref=src.at[to],
                    dst_ref=dst.at[me],
                    send_sem=send_sem,
                    recv_sem=recv_sem,
                    device_id=device_of(to),
                    device_id_type=MESH,
                ).start()

        def landed():
            whole = dst.at[pl.ds(0, n - 1)]
            pltpu.make_async_copy(whole, whole, recv_sem).wait()

        def left():
            whole = src.at[pl.ds(0, n - 1)]
            pltpu.make_async_copy(whole, whole, send_sem).wait()

        return start, landed, left

    def products(level):
        u = u_ref[level]
        v = v_ref[level]
        return jnp.concatenate([u * v, u * u - v * v], axis=1)

    def prepare(level):
        send_l[level] = products(level)

    start, wait, left1 = exchange(send_l, recv_l, sl, rl, in_sector, lon, SECTORS)
    start(prepare)
    recv_l[lon] = products(lon)

    for load in loads[2:6]:
        load.wait()
    ws = ws_ref[...].reshape(1, waves)
    owner = ws // cap
    lane = (owner // (NZ * NC) * NC + owner % NC) * 128 + owner // NC % NZ * cap + ws % cap
    digit = lax.broadcasted_iota(jnp.int32, (16, waves), 0)
    digits = jnp.where(digit == 0, lane // 32, jnp.where(digit == 1, lane % 32, 1)).astype(F32)
    ordered = nn(digits.astype(BF16), order[...])
    target = (ordered[0:1] * 32.0 + ordered[1:2] + ordered[2:3] - 1.0).astype(jnp.int32)
    for b in range(GROUPS):
        ids = lax.broadcasted_iota(jnp.int32, (128, 1024), 0) + b * 128
        onehot[pl.ds(b * 128, 128), :] = jnp.where(ids == target, 1.0, 0.0).astype(BF16)

    rows40 = damp.shape[0]
    slot = lax.broadcasted_iota(jnp.int32, (rows40, waves), 0) // 4
    here = (ws == lat * cap + slot) & (slot < cap)
    wave_ids = lax.broadcasted_iota(jnp.int32, (rows40, waves), 1)
    wave_here = jnp.sum(jnp.where(here, wave_ids, 0).astype(F32), axis=1, keepdims=True)
    kept_here = jnp.sum(jnp.where(here, cnt_ref[...].reshape(1, waves), 0).astype(F32), axis=1, keepdims=True)
    levels = lax.broadcasted_iota(jnp.int32, (1, SECTORS), 1)
    rate = jnp.sum(jnp.where(levels == lon, visc_ref[...].reshape(1, SECTORS), 0.0), axis=1, keepdims=True)
    degree = lax.broadcasted_iota(jnp.int32, (rows40, degrees), 1).astype(F32)
    total = wave_here + degree
    q = total * (total + 1.0) / float(degrees * (degrees + 1))
    damping = (1.0 / math.sqrt(2 * half_lat)) / (1.0 + rate * (q * q))
    damp[...] = jnp.where(degree < kept_here, damping, 0.0)

    wait()
    loads[6].wait()
    loads[7].wait()

    a = [recv_l[s] for s in range(SECTORS)]
    e0, e1, e2, e3 = (a[i] + a[i + 4] for i in range(4))
    o0, o1, o2, o3 = (a[i] - a[i + 4] for i in range(4))
    od = HALF * (o1 - o3)
    os = HALF * (o1 + o3)
    sums = (
        (e0 + e1 + e2 + e3, e0 - e1 + e2 - e3),
        (o0 + od, -(os + o2)),
        (e0 - e2, e3 - e1),
        (o0 - od, o2 - os),
    )
    for j in range(4):
        one, two = sums[j]
        both = jnp.concatenate(
            [
                jnp.concatenate([one[:, :sector], two[:, :sector]], axis=1),
                jnp.concatenate([one[:, sector:], two[:, sector:]], axis=1),
            ],
            axis=0,
        )
        high = both.astype(BF16)
        low = (both - high.astype(F32)).astype(BF16)
        two = nn(jnp.concatenate([high, low], axis=0), hi[j])
        four = two[:32] + two[32:] + nn(high, lo[j])
        turned[0:32, pl.ds(j * 256, 256)] = four[:, :256].astype(BF16)
        turned[32:64, pl.ds(j * 256, 256)] = four[:, 256:].astype(BF16)

    placed = nt(turned[...], onehot[...]).astype(BF16)
    for g in range(GROUPS):
        for b in range(4):
            send_a[g, :, pl.ds(b * 128, 128)] = placed[b * 16 : b * 16 + 16, g * 128 : g * 128 + 128]
    start, wait, left2 = exchange(send_a, recv_a, sa, ra, in_group, group, GROUPS)
    start()
    recv_a[group] = send_a[group]
    loads[8].wait()
    wait()
    arrived = recv_a[...].reshape(GROUPS * 16, 512)
    full = PARTS * NZ * ROWS

    def over_z(src, dst, send_sems, recv_sems, rest_src, rest_dst):
        pieces = [(src.at[p], dst.at[p]) for p in range(PARTS)] + [(rest_src, rest_dst)]
        return [
            exchange(a, b, send_sems.at[p], recv_sems.at[p], in_column, z, NZ)
            for p, (a, b) in enumerate(pieces)
        ]

    there = over_z(send_b, recv_b, sb, rb, send_c, recv_c)
    back = over_z(send_b2, recv_b2, sb2, rb2, send_c2, recv_c2)
    for p in range(PARTS):
        spread = nt(e_tab[pl.ds(p * NZ * ROWS, NZ * ROWS), :], arrived)
        send_b[p] = spread.astype(BF16).reshape(NZ, ROWS, 128)
        there[p][0]()
    spread = nt(e_tab[pl.ds(full, NZ * REST), :], arrived)
    for zz in range(NZ):
        send_c[zz] = spread[REST * zz : REST * zz + REST]
    there[PARTS][0]()
    for p in range(PARTS):
        recv_b[p, z] = send_b[p, z]
    recv_c[z] = send_c[z]
    for load in loads[9:]:
        load.wait()

    quarters = NZ // 4
    parity = jnp.where(lax.broadcasted_iota(jnp.int32, (8, degrees), 1) % 2 == 0, 1.0, -1.0)
    first = lax.broadcasted_iota(jnp.int32, (8, 1), 0) < 4
    blocks = half_lat // 128
    pad = jnp.zeros((ROWS - REST, 512), F32)
    for p in range(PARTS + 1):
        there[p][1]()
        gathered = []
        for i in range(quarters):
            if p < PARTS:
                gathered.append(jnp.concatenate([recv_b[p, 4 * i + k] for k in range(4)], axis=1))
            else:
                rest = jnp.concatenate([recv_c[4 * i + k] for k in range(4)], axis=1)
                gathered.append(jnp.concatenate([rest, pad], axis=0).astype(BF16))
        gathered = jnp.concatenate(gathered, axis=0)
        natural = nn(gathered, pi_tab[...])
        for i in range(2 * p, min(2 * p + 2, (cap + 1) // 2)):
            r0 = 8 * (i - 2 * p)
            north, south = [], []
            for b in range(blocks):
                xx, gg = b // quarters, b % quarters
                north.append(natural[gg * ROWS + r0 : gg * ROWS + r0 + 8, xx * 128 : xx * 128 + 128])
                xx, gg = NX - 1 - xx, quarters - 1 - gg
                south.append(natural[gg * ROWS + r0 : gg * ROWS + r0 + 8, xx * 128 : xx * 128 + 128])
            both = jnp.concatenate(
                [jnp.concatenate(north, axis=1), jnp.concatenate(south, axis=1)], axis=0
            ).astype(BF16)
            raws = []
            for k in (2 * i, 2 * i + 1):
                if k < cap:
                    out = nt(both, basis[k])
                    raws.append(out[:8] + parity * out[8:])
            raw = jnp.where(first, raws[0], raws[1] if len(raws) > 1 else 0.0)
            spectral = raw * damp[pl.ds(8 * i, 8), :]
            for k in (2 * i, 2 * i + 1):
                if k < cap:
                    at = 4 * (k - 2 * i)
                    for f in range(2):
                        spec_ref[k, 0, f] = spectral[at + 2 * f : at + 2 * f + 2]
            rounded = spectral.astype(BF16).astype(F32)
            pair = jnp.concatenate([rounded, rounded * parity], axis=0).astype(BF16)
            outs = [nn(pair, basis[k]) for k in (2 * i, 2 * i + 1) if k < cap]
            keep = jnp.concatenate([first, first], axis=0)
            synth = jnp.where(keep, outs[0], outs[1] if len(outs) > 1 else 0.0)
            synth = synth * (1.0 / math.sqrt(degrees))
            for b in range(blocks):
                xx, gg = b // quarters, b % quarters
                back_t[p, pl.ds(gg * ROWS + r0, 8), pl.ds(xx * 128, 128)] = synth[:8, b * 128 : b * 128 + 128]
                xx, gg = NX - 1 - xx, quarters - 1 - gg
                back_t[p, pl.ds(gg * ROWS + r0, 8), pl.ds(xx * 128, 128)] = synth[8:, b * 128 : b * 128 + 128]
        for gg in range(quarters):
            if 2 * p + 2 > (cap + 1) // 2:
                back_t[p, pl.ds(gg * ROWS + 8, 8), :] = jnp.zeros((8, 512), F32)
        mixed = nn(back_t[p].astype(BF16), pi_t[...])
        for zz in range(NZ):
            piece = mixed[zz // 4 * ROWS : zz // 4 * ROWS + ROWS, zz % 4 * 128 : zz % 4 * 128 + 128]
            if p < PARTS:
                send_b2[p, zz] = piece.astype(BF16)
            else:
                send_c2[zz] = piece[:REST]
        back[p][0]()
        if p < PARTS:
            recv_b2[p, z] = send_b2[p, z]
        else:
            recv_c2[z] = send_c2[z]

    joined = 0.0
    for p in range(PARTS):
        back[p][1]()
        rows = NZ * ROWS
        joined += tn(recv_b2[p].reshape(rows, 128), e_tab[pl.ds(p * rows, rows), :])
    back[PARTS][1]()
    rest = jnp.concatenate([recv_c2[zz] for zz in range(NZ)], axis=0).astype(BF16)
    joined += tn(rest, e_tab[pl.ds(full, NZ * REST), :])
    send_a2[...] = joined.astype(BF16).reshape(GROUPS, 16, 512)
    start, wait, left5 = exchange(send_a2, recv_a2, sa2, ra2, in_group, group, GROUPS)
    start()
    recv_a2[group] = send_a2[group]
    wait()

    by_part = jnp.concatenate(
        [
            jnp.concatenate([recv_a2[g, :, pl.ds(b * 128, 128)] for g in range(GROUPS)], axis=1)
            for b in range(4)
        ],
        axis=0,
    )
    waved = nn(by_part, onehot[...])
    weight = jnp.where(lax.broadcasted_iota(jnp.int32, (1, 1024), 1) == 0, 1.0, 2.0)
    waved = (waved * weight).astype(BF16)
    parts = []
    for j in range(4):
        lhs = jnp.concatenate(
            [waved[:32, j * 256 : j * 256 + 256], waved[32:, j * 256 : j * 256 + 256]], axis=1
        )
        out = nn(lhs, hi_t[j])
        parts.append((out[:, :sector], out[:, sector:]))
    (u0, u4), (u1, v1), (u2, v2), (u3, v3) = parts
    even, odd = u0 + u4, u0 - u4
    ud, us = HALF * (u1 - u3), u1 + u3
    vd, vs = v1 - v3, HALF * (v1 + v3)
    grid = (
        even + us + u2,
        odd + ud - vs - v2,
        even - u2 - vd,
        odd - ud - vs + v2,
        even - us + u2,
        odd - ud + vs - v2,
        even - u2 + vd,
        odd + ud + vs + v2,
    )
    for s in range(SECTORS):
        send_l2[s] = jnp.concatenate([grid[s][:16], grid[s][16:]], axis=1).astype(BF16)
    start, wait, left6 = exchange(send_l2, recv_l2, sl2, rl2, in_sector, lon, SECTORS)
    start()
    recv_l2[lon] = send_l2[lon]
    wait()
    for s in range(SECTORS):
        both = recv_l2[s].astype(F32)
        tend_ref[s, 0] = both[:, :sector]
        tend_ref[s, 1] = both[:, sector:]
    for left in (left1, left2, left5, left6, *(e[2] for e in there), *(e[2] for e in back)):
        left()


def body(wind_u, wind_v, basis, wave_slots, degree_count, viscosity):
    levels, lat_rows, sector = wind_u.shape
    cap, degrees, half_lat = basis.shape
    waves = wave_slots.shape[0]
    high, low = dft_table(sector * SECTORS, waves)
    vmem = pl.BlockSpec(memory_space=pltpu.VMEM)
    hbm = pl.BlockSpec(memory_space=pltpu.HBM)
    dma = pltpu.SemaphoreType.DMA
    return pl.pallas_call(
        kernel,
        out_shape=(
            jax.ShapeDtypeStruct((cap, 1, 2, 2, degrees), F32),
            jax.ShapeDtypeStruct((levels, 2, lat_rows, sector), F32),
        ),
        in_specs=[hbm] * 13,
        out_specs=(vmem, vmem),
        scratch_shapes=[
            pltpu.VMEM(wind_u.shape, F32),
            pltpu.VMEM(wind_v.shape, F32),
            pltpu.VMEM((waves,), jnp.int32),
            pltpu.VMEM((waves,), jnp.int32),
            pltpu.VMEM((levels,), F32),
            pltpu.VMEM((waves, 1024), BF16),
            pltpu.VMEM(basis.shape, BF16),
            pltpu.VMEM(high.shape, BF16),
            pltpu.VMEM(low.shape, BF16),
            pltpu.VMEM((PARTS * NZ * ROWS + NZ * REST, 512), BF16),
            pltpu.VMEM((512, 512), BF16),
            pltpu.VMEM((high.shape[0], high.shape[2], high.shape[1]), BF16),
            pltpu.VMEM((512, 512), BF16),
            pltpu.VMEM((1024, 1024), BF16),
            pltpu.VMEM((40, degrees), F32),
            pltpu.VMEM((SECTORS, lat_rows, 2 * sector), F32),
            pltpu.VMEM((SECTORS, lat_rows, 2 * sector), F32),
            pltpu.VMEM((GROUPS, 16, 512), BF16),
            pltpu.VMEM((GROUPS, 16, 512), BF16),
            pltpu.VMEM((PARTS, NZ, ROWS, 128), BF16),
            pltpu.VMEM((PARTS, NZ, ROWS, 128), BF16),
            pltpu.VMEM((64, 1024), BF16),
            pltpu.VMEM((PARTS + 1, NZ // 4 * ROWS, 512), F32),
            pltpu.VMEM((PARTS, NZ, ROWS, 128), BF16),
            pltpu.VMEM((PARTS, NZ, ROWS, 128), BF16),
            pltpu.VMEM((NZ, REST, 128), F32),
            pltpu.VMEM((NZ, REST, 128), F32),
            pltpu.VMEM((NZ, REST, 128), F32),
            pltpu.VMEM((NZ, REST, 128), F32),
            pltpu.VMEM((GROUPS, 16, 512), BF16),
            pltpu.VMEM((GROUPS, 16, 512), BF16),
            pltpu.VMEM((SECTORS, lat_rows, 2 * sector), BF16),
            pltpu.VMEM((SECTORS, lat_rows, 2 * sector), BF16),
            dma((13,)),
        ]
        + [dma(())] * 4 + [dma((PARTS + 1,))] * 4 + [dma(())] * 4,
        compiler_params=pltpu.CompilerParams(
            collective_id=0, has_side_effects=True, vmem_limit_bytes=40 * 2**20
        ),
    )(
        *(
            pltpu.with_memory_space_constraint(operand, pltpu.HBM)
            for operand in (
                wind_u,
                wind_v,
                wave_slots,
                degree_count,
                viscosity,
                basis,
                jnp.asarray(high),
                jnp.asarray(low),
                jnp.asarray(spread_table(cap)),
                jnp.asarray(lane_table()),
                jnp.asarray(order_table(waves)),
                jnp.asarray(np.ascontiguousarray(high.transpose(0, 2, 1))),
                jnp.asarray(np.ascontiguousarray(lane_table().T)),
            )
        )
    )


def solution(mesh):
    return jax.shard_map(
        body,
        mesh=mesh,
        in_specs=(
            P(None, "lat", "lon"),
            P(None, "lat", "lon"),
            P("lat", None, None),
            P(),
            P(),
            P(),
        ),
        out_specs=(P("lat", "lon", None, None, None), P(None, None, "lat", "lon")),
        check_vma=False,
    )
```
